256 devices in a mesh: sec: 4 (over x_hi, core), dev: 64 (over z, y, x_lo).
Axes of the slice: x: 4 (x_hi: 2, x_lo: 2; x = x_hi * 2 + x_lo), y: 4, z: 8, core: 2. Of those that a mesh axis runs over, the one named last changes fastest.
Arguments:
- user_features: bfloat16 [262144, 1024], P(('sec', 'dev')), may hold values from -6 to 6
- w_query_in: bfloat16 [1024, 1024], replicated, may hold values from -0.1875 to 0.1875
- w_query_out: bfloat16 [1024, 256], replicated, may hold values from -0.1875 to 0.1875
- quo_table: bfloat16 [8192, 1024], P('dev'), may hold values from -6 to 6
- rem_table: bfloat16 [8192, 1024], P('dev'), may hold values from -6 to 6
- w_item_in: bfloat16 [1024, 1024], replicated, may hold values from -0.1875 to 0.1875
- w_item_out: bfloat16 [1024, 256], replicated, may hold values from -0.1875 to 0.1875
- quo_bucket: int32 [2048], P('dev'), may hold values from 0 to 8191
- rem_bucket: int32 [2048], P('dev'), may hold values from 0 to 8191
- counts: int32 [2048], replicated, may hold values from 1 to 1000
- positive: int32 [262144], P(('sec', 'dev')), may hold values from 0 to 2047
Outputs:
- losses: float32 [262144], P(('sec', 'dev'))
- grad_query_out: float32 [1024, 256], replicated
- grad_item_out: float32 [1024, 256], replicated
The draws below stay inside these ranges and needn't reach their ends.
All inputs are finite; a program needn't handle non-finite values.
Results may differ from the reference program's by a relative error of at most 0.004.
The reference program's roundings to bfloat16 on the way count: a program that leaves them out, or rounds other values in their place, can miss the bound.
Values may be sent and summed in bfloat16 or wider, within the bound.
A program may use at most 128 MiB of HBM per device.

```python
import jax
import jax.numpy as jnp
from jax import lax

DIN = 1024
HID = 1024
DOUT = 256
EMB = 1024
TOK_DEV = 1024
QUERIES = 262144
ITEMS = 2048
TROWS = 8192


def place_ends(drawn, key, least, largest):
    place = [jax.random.randint(jax.random.fold_in(key, axis), (), 0, length) for axis, length in enumerate(drawn.shape)]
    longest = drawn.shape.index(max(drawn.shape))
    neighbour = place[:longest] + [(place[longest] + 1) % drawn.shape[longest]] + place[longest + 1:]
    return drawn.at[tuple(place)].set(least).at[tuple(neighbour)].set(largest)


def levels(own_key, dims, cuts, smallest, largest):
    def one(dim, shards_of):
        steps = jax.random.uniform(jax.random.fold_in(jax.random.fold_in(own_key, 6), dim), (shards_of,), jnp.float32, smallest / len(cuts), largest / len(cuts))
        return jnp.repeat(jnp.exp(steps), dims[dim] // shards_of).reshape((-1,) + (1,) * (len(dims) - dim - 1))

    factor_of = one(*cuts[0])
    for cut in cuts[1:]:
        factor_of = factor_of * one(*cut)
    return factor_of


def scatter_about(rng, shape, scale, bound, split=(), held_as=jnp.bfloat16):
    factor_of = levels(rng, shape, split, -0.22, 0.18) if split else 1.0
    values = jax.random.normal(rng, shape, jnp.float32) * scale * factor_of
    return jnp.minimum(jnp.maximum(values, -bound), bound).astype(held_as)


def setup_inputs(seed: int = 0) -> dict:
    key_of = jax.random.split(jax.random.key(seed), 12)
    user_features = scatter_about(key_of[0], (QUERIES, DIN), 1.0, 6.0, ((0, 256),))
    w_query_in = scatter_about(key_of[1], (DIN, HID), DIN ** -0.5, 0.1875)
    w_query_out = scatter_about(key_of[2], (HID, DOUT), HID ** -0.5, 0.1875)
    quo_table = scatter_about(key_of[3], (TROWS, EMB), 1.0, 6.0, ((0, 64),))
    rem_table = scatter_about(key_of[4], (TROWS, EMB), 1.0, 6.0, ((0, 64),))
    w_item_in = scatter_about(key_of[5], (EMB, HID), EMB ** -0.5, 0.1875)
    w_item_out = scatter_about(key_of[6], (HID, DOUT), HID ** -0.5, 0.1875)
    quo_bucket = place_ends(jax.random.randint(key_of[7], (ITEMS,), 0, TROWS), jax.random.fold_in(key_of[7], 1), 0, TROWS - 1).astype(jnp.int32)
    rem_bucket = place_ends(jax.random.randint(key_of[8], (ITEMS,), 0, TROWS), jax.random.fold_in(key_of[8], 1), 0, TROWS - 1).astype(jnp.int32)
    counts = place_ends(jax.random.randint(key_of[9], (ITEMS,), 1, 1001), jax.random.fold_in(key_of[9], 1), 1, 1000).astype(jnp.int32)
    positive = place_ends(jax.random.randint(key_of[10], (QUERIES,), 0, ITEMS), jax.random.fold_in(key_of[10], 1), 0, ITEMS - 1).astype(jnp.int32)
    return dict(user_features=user_features, w_query_in=w_query_in, w_query_out=w_query_out, quo_table=quo_table, rem_table=rem_table, w_item_in=w_item_in, w_item_out=w_item_out, quo_bucket=quo_bucket, rem_bucket=rem_bucket, counts=counts, positive=positive)


epsilon = 1e-06
softmax_temper = 0.05

def normalize(vectors):
    width = vectors.shape[-1]
    return vectors * lax.rsqrt(lax.optimization_barrier(jnp.mean(vectors * vectors, axis=-1, keepdims=True)) + epsilon) * width ** (-0.5)

def reference(user_features, w_query_in, w_query_out, quo_table, rem_table, w_item_in, w_item_out, quo_bucket, rem_bucket, counts, positive):
    embedded = (quo_table[quo_bucket].astype(jnp.float32) * rem_table[rem_bucket].astype(jnp.float32)).astype(jnp.bfloat16)
    hidden_item = jax.nn.relu(jnp.dot(embedded, w_item_in, preferred_element_type=jnp.float32)).astype(jnp.bfloat16)
    item_raw = jnp.dot(hidden_item, w_item_out, preferred_element_type=jnp.float32)
    item_embedding_rows = normalize(item_raw).astype(jnp.bfloat16)
    log_frequency = jnp.log(counts.astype(jnp.float32))
    feature_blocks = user_features.reshape(-1, TOK_DEV, DIN)
    positive_blocks = positive.reshape(-1, TOK_DEV)
    item_index = jnp.arange(ITEMS, dtype=jnp.int32)

    def block_step(totals, inputs):
        query_total, item_grand_count = totals
        features, targets = inputs
        hidden_query = jax.nn.relu(jnp.dot(features, w_query_in, preferred_element_type=jnp.float32)).astype(jnp.bfloat16)
        query_raw = jnp.dot(hidden_query, w_query_out, preferred_element_type=jnp.float32)
        query_embedding_rows = normalize(query_raw).astype(jnp.bfloat16)
        logit_matrix = jnp.dot(query_embedding_rows, item_embedding_rows.T, preferred_element_type=jnp.float32) / softmax_temper - log_frequency[None, :]
        log_total = jnp.log(lax.optimization_barrier(jnp.sum(jnp.exp(logit_matrix), axis=1)))
        picked = jnp.take_along_axis(logit_matrix, targets[:, None], axis=1)[:, 0]
        block_losses = log_total - picked
        probs = jnp.exp(logit_matrix - log_total[:, None])
        onehot = (item_index[None, :] == targets[:, None]).astype(jnp.float32)
        logit_gradient = (probs - onehot).astype(jnp.bfloat16)
        query_gradient = jnp.dot(logit_gradient, item_embedding_rows, preferred_element_type=jnp.float32) / softmax_temper
        _, pullback = jax.vjp(normalize, query_raw)
        raw_grad = pullback(query_gradient)[0].astype(jnp.bfloat16)
        query_total = query_total + jnp.dot(hidden_query.T, raw_grad, preferred_element_type=jnp.float32)
        item_grand_count = item_grand_count + jnp.dot(logit_gradient.T, query_embedding_rows, preferred_element_type=jnp.float32) / softmax_temper
        return ((query_total, item_grand_count), block_losses)
    start_totals = (jnp.zeros((HID, DOUT), jnp.float32), jnp.zeros((ITEMS, DOUT), jnp.float32))
    (query_total, item_grand_count), losses = lax.scan(block_step, start_totals, (feature_blocks, positive_blocks))
    _, pullback = jax.vjp(normalize, item_raw)
    item_raw_grad = pullback(item_grand_count)[0].astype(jnp.bfloat16)
    item_grad = jnp.dot(hidden_item.T, item_raw_grad, preferred_element_type=jnp.float32)
    limit = (HID * DOUT / 2) ** 0.5
    grad_norm = jnp.sqrt(jnp.sum(query_total * query_total) + jnp.sum(item_grad * item_grad))
    factor = limit / jnp.maximum(grad_norm, limit)
    return (losses.reshape(-1), query_total * factor, item_grad * factor)
```

```python
import jax
import jax.numpy as jnp
from jax import lax
from jax.experimental import pallas as pl
from jax.experimental.pallas import tpu as pltpu
from jax.sharding import PartitionSpec as P

EPS = 1e-06
INV_TEMPER = 20.0
MESH = pl.DeviceIdType.MESH
F32 = jnp.float32
BF16 = jnp.bfloat16

NX, NC, NY, NZ = 4, 2, 4, 8
PLANE = NY * NZ
TOK, DIN, HID, DOUT = 1024, 1024, 1024, 256
QUARTER = 8
BLOCK = PLANE * QUARTER
SLOTS = NX * NC
SHARD = 128
TROWS = 8192
CHUNKS = 4
WIDE = DIN // CHUNKS
TILE = 256


def dot(a, b, ca, cb):
    return lax.dot_general(a, b, (((ca,), (cb,)), ((), ())), preferred_element_type=F32)


def norm_parts(raw):
    r = lax.rsqrt(jnp.mean(raw * raw, axis=-1, keepdims=True) + EPS)
    return r


def norm_vjp(raw, grad):
    r = norm_parts(raw)
    dotted = jnp.mean(grad * raw, axis=-1, keepdims=True)
    return (grad * r - raw * (r * r * r * dotted)) * (DOUT**-0.5)


def kernel(
    idx_in, feat_hbm, wqi_hbm, wqo_hbm, quo_hbm, rem_hbm, wii_hbm, wio_hbm, lc_ref, pos_ref,
    loss_ref, gq_ref, gi_ref,
    feat, wqi, wqo, tab, wii, wio,
    idx_recv, idx_sum, srow, rrow, zrow, rzrow,
    hq, qraw, qv, xall, gz, hz, h256,
    est, esum, psum, inv_ref, gall, tsrc, rc, sx, rx, sy, ry, sz, rz,
    rgz, rgy, araw, asrc, arc, asx, arx,
    qsrc, qrc, qsx, qrx, qsy, qry, qz, qy,
    fin, nrm,
    load_sem,
    idx_ss, idx_rs, tab_ss, tab_rs, ry_ss, ry_rs, rz_ss, rz_rs,
    vz_ss, vz_rs, vy_ss, vy_rs, vx_ss, vx_rs, vc_ss, vc_rs,
    hz_ss, hz_rs, hy_ss, hy_rs,
    tc_ss, tc_rs, tx_ss, tx_rs, ty_ss, ty_rs, tz_ss, tz_rs,
    gz_ss, gz_rs, gy_ss, gy_rs,
    ac_ss, ac_rs, ax_ss, ax_rs,
    qc_ss, qc_rs, qx_ss, qx_rs, qyr_ss, qyr_rs, qz_ss, qz_rs, qyg_ss, qyg_rs,
    fx_ss, fx_rs, fc_ss, fc_rs, n_ss, n_rs,
):
    sec = lax.axis_index("sec")
    dev = lax.axis_index("dev")
    xh, c = sec // 2, sec % 2
    z, y, xl = dev // 8, (dev // 2) % 4, dev % 2
    x = xh * 2 + xl
    slot = x * 2 + c
    oc = 1 - c

    def at(ax, ac, ay, az):
        return ((ax // 2) * 2 + ac, (az * NY + ay) * 2 + ax % 2)

    def zp(k):
        return at(x, c, y, (z + k) % NZ)

    def yp(k):
        return at(x, c, (y + k) % NY, z)

    def xp(k):
        return at((x + k) % NX, c, y, z)

    other = at(x, oc, y, z)
    plane = [(ky, kz) for ky in range(NY) for kz in range(NZ) if ky or kz]
    column = [(kx, kc) for kx in range(NX) for kc in range(NC) if kx or kc]
    partner_x = jnp.where(c == 0, x + 1 - 2 * (x % 2), (x + 3 + 2 * (x % 2)) % NX)
    partner = at(partner_x, c, y, z)

    def push(src, dst, ss, rs, target):
        cp = pltpu.make_async_remote_copy(
            src_ref=src, dst_ref=dst, send_sem=ss, recv_sem=rs, device_id=target, device_id_type=MESH
        )
        cp.start()
        return cp

    barrier = pltpu.get_barrier_semaphore()
    for ky, kz in plane:
        pl.semaphore_signal(
            barrier, inc=1, device_id=at(x, c, (y + ky) % NY, (z + kz) % NZ), device_id_type=MESH
        )
    for kx, kc in column:
        pl.semaphore_signal(
            barrier, inc=1, device_id=at((x + kx) % NX, (c + kc) % NC, y, z), device_id_type=MESH
        )

    loads = []
    for i, (src, dst) in enumerate(
        [
            (quo_hbm, tab.at[0]),
            (rem_hbm, tab.at[2]),
            (feat_hbm, feat),
            (wqi_hbm, wqi),
            (wqo_hbm, wqo),
            (wii_hbm, wii),
            (wio_hbm, wio),
        ]
    ):
        cp = pltpu.make_async_copy(src, dst, load_sem.at[i])
        cp.start()
        loads.append(cp)
    pl.semaphore_wait(barrier, len(plane) + len(column))

    idx_cp = []
    for i, (ky, kz) in enumerate(plane):
        idx_cp.append(
            push(
                idx_in,
                idx_recv.at[i],
                idx_ss.at[i],
                idx_rs.at[i],
                at(x, c, (y + ky) % NY, (z + kz) % NZ),
            )
        )
    tab_cp = [
        push(quo_hbm, tab.at[1], tab_ss.at[0], tab_rs.at[0], partner),
        push(rem_hbm, tab.at[3], tab_ss.at[1], tab_rs.at[1], partner),
    ]

    loads[2].wait()
    loads[3].wait()
    for r in range(TOK // TILE):
        rows = pl.ds(r * TILE, TILE)

        @pl.loop(0, HID // TILE)
        def _(j):
            cols = pl.ds(pl.multiple_of(j * TILE, TILE), TILE)
            h = dot(feat[rows, :], wqi[:, cols], 1, 0)
            hq[rows, cols] = jnp.maximum(h, 0.0).astype(BF16)

    for cp in idx_cp:
        cp.wait()
    total = idx_in[...]
    for i in range(len(plane)):
        total = total + idx_recv[i]
    idx_sum[...] = total
    loads[0].wait()
    loads[1].wait()
    for cp in tab_cp:
        cp.wait()
    line = lax.broadcasted_iota(jnp.int32, (4 * SHARD, 128), 0)
    which = line // SHARD
    pair_dev = dev + 1 - 2 * xl
    owner = jnp.where(which % 2 == 0, dev, pair_dev)
    row_id = line % SHARD + owner * SHARD + (which // 2) * TROWS
    tables = tab[...].reshape(4 * SHARD, DIN)

    row_cp = [[None] * NY for _ in range(CHUNKS)]
    for k in (1, 3, 2, 0):
        yy = (y + k) % NY
        wanted = idx_sum[pl.ds(yy, 1), :]
        sel = (row_id == wanted).astype(F32).astype(BF16)
        for ch in range(CHUNKS):
            got = dot(sel, tables[:, ch * WIDE : (ch + 1) * WIDE], 0, 0)
            srow[ch, k] = got.astype(BF16)
    for ch in range(CHUNKS):
        for k in (1, 3, 2):
            row_cp[ch][k] = push(
                srow.at[ch, k], rrow.at[ch, k - 1], ry_ss.at[ch, k - 1], ry_rs.at[ch, k - 1], yp(k)
            )

    loads[4].wait()
    for r in range(TOK // TILE):
        rows = pl.ds(r * TILE, TILE)
        raw = dot(hq[rows, :], wqo[...], 1, 0)
        qraw[rows, :] = raw
        qv[rows, :] = (raw * norm_parts(raw) * (DOUT**-0.5)).astype(BF16)

    zrow_cp = [[None] * NZ for _ in range(CHUNKS)]
    for ch in range(CHUNKS):
        for k in (1, 3, 2):
            row_cp[ch][k].wait()
        s = srow[ch, 0].astype(F32)
        for k in range(NY - 1):
            s = s + rrow[ch, k].astype(F32)
        zrow[ch] = s.astype(BF16).reshape(NZ, 16, WIDE)
        for k in range(1, NZ):
            zrow_cp[ch][k] = push(
                zrow.at[ch, (z + k) % NZ],
                rzrow.at[ch, k - 1],
                rz_ss.at[ch, k - 1],
                rz_rs.at[ch, k - 1],
                zp(k),
            )

    loads[5].wait()
    loads[6].wait()
    pre = jnp.zeros((16, HID), F32)
    for ch in range(CHUNKS):
        for k in range(1, NZ):
            zrow_cp[ch][k].wait()
        s = zrow[ch, z].astype(F32)
        for k in range(NZ - 1):
            s = s + rzrow[ch, k].astype(F32)
        emb = s[:8] * s[8:]
        emb = jnp.concatenate([emb, emb], axis=0).astype(BF16)
        pre = pre + dot(emb, wii[ch * WIDE : (ch + 1) * WIDE, :], 1, 0)
    hid = jnp.maximum(pre, 0.0).astype(BF16)
    iraw = dot(hid, wio[...], 1, 0)[:8]
    ivec = (iraw * norm_parts(iraw) * (DOUT**-0.5)).astype(BF16).astype(F32)
    gz[z] = ivec

    v_cp = []
    for k in range(1, NZ):
        v_cp.append(push(gz.at[z], gz.at[z], vz_ss.at[k - 1], vz_rs.at[k - 1], zp(k)))
    hid8 = hid.astype(F32)[:8]
    hz[z] = jnp.concatenate([hid8[:, :512], hid8[:, 512:]], axis=0).astype(BF16)
    hz_cp = []
    for k in range(1, NZ):
        hz_cp.append(push(hz.at[z], hz.at[z], hz_ss.at[k - 1], hz_rs.at[k - 1], zp(k)))
    for cp in v_cp:
        cp.wait()
    xall[slot, y] = gz[...].reshape(64, DOUT).astype(BF16)
    v_cp = []
    for k in range(1, NY):
        v_cp.append(push(xall.at[slot, y], xall.at[slot, y], vy_ss.at[k - 1], vy_rs.at[k - 1], yp(k)))
    for cp in v_cp:
        cp.wait()
    vx_cp = [None]
    for k in (1, 3, 2):
        vx_cp.append(push(xall.at[slot], xall.at[slot], vx_ss.at[k - 1], vx_rs.at[k - 1], xp(k)))
    vx_cp = [None, vx_cp[1], vx_cp[3], vx_cp[2]]
    vc_cp = [push(xall.at[slot], xall.at[slot], vc_ss.at[0], vc_rs.at[0], other)]

    esum[...] = jnp.zeros_like(esum)
    psum[...] = jnp.zeros_like(psum)

    def first_pass(s):
        vec = xall[s].reshape(BLOCK, DOUT)
        log_count = lc_ref[s]

        @pl.loop(0, TOK // TILE)
        def _(r):
            rows = pl.ds(pl.multiple_of(r * TILE, TILE), TILE)
            logit = dot(qv[rows, :], vec, 1, 1) * INV_TEMPER - log_count
            e = jnp.exp(logit)
            est[s, rows, :] = e
            esum[rows, :] += e[:, :128] + e[:, 128:]
            lane = lax.broadcasted_iota(jnp.int32, (TILE, BLOCK), 1) + s * BLOCK
            hit = jnp.where(lane == pos_ref[rows, :], logit, 0.0)
            psum[rows, :] += hit[:, :128] + hit[:, 128:]

    first_pass(slot)
    vc_cp[0].wait()
    first_pass(x * 2 + oc)
    for i, k in enumerate((1, 3, 2)):
        vx_cp[k].wait()
        s = ((x + NX - k) % NX) * 2 + c
        cp = push(xall.at[s], xall.at[s], vc_ss.at[i + 1], vc_rs.at[i + 1], other)
        vc_cp.append(cp)
        first_pass(s)
        cp.wait()
        first_pass(((x + NX - k) % NX) * 2 + oc)

    for cp in hz_cp:
        cp.wait()
    hv = hz[...].astype(F32)
    h256[y, :, :512] = hv[:, :8, :].reshape(64, 512).astype(BF16)
    h256[y, :, 512:] = hv[:, 8:, :].reshape(64, 512).astype(BF16)
    hy_cp = []

    sums = jnp.sum(esum[...], axis=1, keepdims=True)
    picked = jnp.sum(psum[...], axis=1, keepdims=True)
    loss_ref[...] = jnp.log(sums) - picked
    inv_ref[...] = 1.0 / sums

    def second_pass(s):
        @pl.loop(0, TOK // TILE)
        def _(r):
            rows = pl.ds(pl.multiple_of(r * TILE, TILE), TILE)
            p = est[s, rows, :] * inv_ref[rows, :]
            lane = lax.broadcasted_iota(jnp.int32, (TILE, BLOCK), 1) + s * BLOCK
            g = jnp.where(lane == pos_ref[rows, :], p - 1.0, p)
            gall[s, rows, :] = g.astype(BF16)

        return dot(gall[s], qv[...], 0, 0) * INV_TEMPER

    tc_cp = [None] * NX
    for k in (1, 3, 2, 0):
        s = ((x + k) % NX) * 2 + oc
        tsrc[k] = second_pass(s).astype(BF16)
        tc_cp[k] = push(tsrc.at[k], rc.at[k], tc_ss.at[k], tc_rs.at[k], other)
    tx_cp = []
    own = None
    for k in (1, 3, 2, 0):
        t = second_pass(((x + k) % NX) * 2 + c)
        tc_cp[k].wait()
        t = t + rc[k].astype(F32)
        if k:
            sx[k - 1] = t.astype(BF16)
            tx_cp.append(push(sx.at[k - 1], rx.at[k - 1], tx_ss.at[k - 1], tx_rs.at[k - 1], xp(k)))
        else:
            own = t
    sx[3] = own.astype(BF16)

    for k in range(1, NY):
        hy_cp.append(push(h256.at[y], h256.at[y], hy_ss.at[k - 1], hy_rs.at[k - 1], yp(k)))

    @pl.loop(0, TOK // TILE)
    def _(r):
        rows = pl.ds(pl.multiple_of(r * TILE, TILE), TILE)
        acc = jnp.zeros((TILE, DOUT), F32)
        for s in range(SLOTS):
            acc = acc + dot(gall[s, rows, :], xall[s].reshape(BLOCK, DOUT), 1, 0)
        qv[rows, :] = norm_vjp(qraw[rows, :], acc * INV_TEMPER).astype(BF16)

    def query_part(half):
        return dot(hq[:, pl.ds(pl.multiple_of(half * 512, 512), 512)], qv[...], 0, 0)

    qsrc[...] = query_part(oc).astype(BF16)
    qc_cp = push(qsrc, qrc, qc_ss.at[0], qc_rs.at[0], other)
    qown = query_part(c)

    for cp in tx_cp:
        cp.wait()
    t = sx[3].astype(F32)
    for k in range(NX - 1):
        t = t + rx[k].astype(F32)
    sy[...] = t.astype(BF16).reshape(NY, 64, DOUT)
    ty_cp = []
    for k in range(1, NY):
        ty_cp.append(push(sy.at[(y + k) % NY], ry.at[k - 1], ty_ss.at[k - 1], ty_rs.at[k - 1], yp(k)))

    qc_cp.wait()
    qown = qown + qrc[...].astype(F32)
    qsx[...] = qown.astype(BF16).reshape(NX, 128, DOUT)
    qx_cp = []
    for k in range(1, NX):
        qx_cp.append(push(qsx.at[(x + k) % NX], qrx.at[k - 1], qx_ss.at[k - 1], qx_rs.at[k - 1], xp(k)))

    for cp in ty_cp:
        cp.wait()
    t = sy[y].astype(F32)
    for k in range(NY - 1):
        t = t + ry[k].astype(F32)
    sz[...] = t.reshape(NZ, 8, DOUT)
    tz_cp = []
    for k in range(1, NZ):
        tz_cp.append(push(sz.at[(z + k) % NZ], rz.at[k - 1], tz_ss.at[k - 1], tz_rs.at[k - 1], zp(k)))

    for cp in qx_cp:
        cp.wait()
    q = qsx[x].astype(F32)
    for k in range(NX - 1):
        q = q + qrx[k].astype(F32)
    qsy[...] = q.astype(BF16).reshape(NY, 32, DOUT)
    qy_cp = []
    for k in range(1, NY):
        qy_cp.append(
            push(qsy.at[(y + k) % NY], qry.at[k - 1], qyr_ss.at[k - 1], qyr_rs.at[k - 1], yp(k))
        )

    for cp in tz_cp:
        cp.wait()
    t = sz[z]
    for k in range(NZ - 1):
        t = t + rz[k]
    rgz[z] = norm_vjp(iraw, t).astype(BF16).astype(F32)
    g_cp = []
    for k in range(1, NZ):
        g_cp.append(push(rgz.at[z], rgz.at[z], gz_ss.at[k - 1], gz_rs.at[k - 1], zp(k)))

    for cp in qy_cp:
        cp.wait()
    q = qsy[y].astype(F32)
    for k in range(NY - 1):
        q = q + qry[k].astype(F32)
    qz[z] = q.astype(BF16)
    qz_cp = []
    for k in range(1, NZ):
        qz_cp.append(push(qz.at[z], qz.at[z], qz_ss.at[k - 1], qz_rs.at[k - 1], zp(k)))

    for cp in g_cp:
        cp.wait()
    rgy[y] = rgz[...].reshape(64, DOUT).astype(BF16)
    g_cp = []
    for k in range(1, NY):
        g_cp.append(push(rgy.at[y], rgy.at[y], gy_ss.at[k - 1], gy_rs.at[k - 1], yp(k)))

    for cp in qz_cp:
        cp.wait()
    q = qz[0].astype(F32)
    for k in range(1, NZ):
        q = q + qz[k].astype(F32)
    qy[y] = q.astype(BF16)
    qy_cp = []
    for k in range(1, NY):
        qy_cp.append(push(qy.at[y], qy.at[y], qyg_ss.at[k - 1], qyg_rs.at[k - 1], yp(k)))

    for cp in hy_cp:
        cp.wait()
    for cp in g_cp:
        cp.wait()
    rg = rgy[...].reshape(BLOCK, DOUT)

    def item_part(half):
        cols = pl.ds(pl.multiple_of(half * 512, 512), 512)
        return dot(h256[:, :, cols].reshape(BLOCK, 512), rg, 0, 0)

    asrc[...] = item_part(oc).astype(BF16)
    ac_cp = push(asrc, arc, ac_ss.at[0], ac_rs.at[0], other)
    araw[...] = item_part(c)
    ac_cp.wait()
    asx[...] = (araw[...] + arc[...].astype(F32)).astype(BF16).reshape(NX, 128, DOUT)
    ax_cp = []
    for k in range(1, NX):
        ax_cp.append(push(asx.at[(x + k) % NX], arx.at[k - 1], ax_ss.at[k - 1], ax_rs.at[k - 1], xp(k)))
    for cp in qy_cp:
        cp.wait()
    fin[slot, 0] = qy[...].reshape(128, DOUT)
    for cp in ax_cp:
        cp.wait()
    a = asx[x].astype(F32)
    for k in range(NX - 1):
        a = a + arx[k].astype(F32)
    fin[slot, 1] = a.astype(BF16)
    mine = fin[slot].astype(F32)
    square = mine * mine
    square = jnp.sum(square.reshape(2 * 128 // 8, 8, DOUT), axis=0)
    nrm[slot] = square[:, :128] + square[:, 128:]

    fx_cp = [None] * NX
    for k in (1, 3, 2):
        fx_cp[k] = push(fin.at[slot], fin.at[slot], fx_ss.at[k - 1], fx_rs.at[k - 1], xp(k))
    n_cp = []
    for i, (kx, kc) in enumerate(column):
        n_cp.append(
            push(
                nrm.at[slot], nrm.at[slot], n_ss.at[i], n_rs.at[i],
                at((x + kx) % NX, (c + kc) % NC, y, z),
            )
        )
    fc_cp = [push(fin.at[slot], fin.at[slot], fc_ss.at[0], fc_rs.at[0], other)]
    for cp in n_cp:
        cp.wait()
    square = nrm[0]
    for s in range(1, SLOTS):
        square = square + nrm[s]
    norm = jnp.sqrt(jnp.sum(jnp.sum(square, axis=1, keepdims=True), axis=0, keepdims=True))
    limit = (HID * DOUT / 2) ** 0.5
    factor = limit / jnp.maximum(norm, limit)

    def put(s):
        at_row = pl.ds(pl.multiple_of((s % 2) * 512 + (s // 2) * 128, 128), 128)
        gq_ref[at_row, :] = fin[s, 0].astype(F32) * factor
        gi_ref[at_row, :] = fin[s, 1].astype(F32) * factor

    put(slot)
    for i, k in enumerate((1, 3, 2)):
        fx_cp[k].wait()
        s = ((x + NX - k) % NX) * 2 + c
        fc_cp.append(push(fin.at[s], fin.at[s], fc_ss.at[i + 1], fc_rs.at[i + 1], other))
        put(s)
    fc_cp[0].wait()
    put(x * 2 + oc)
    for i, k in enumerate((1, 3, 2)):
        fc_cp[i + 1].wait()
        put(((x + NX - k) % NX) * 2 + oc)


def local(
    user_features, w_query_in, w_query_out, quo_table, rem_table, w_item_in, w_item_out,
    quo_bucket, rem_bucket, counts, positive,
):
    sec = lax.axis_index("sec")
    dev = lax.axis_index("dev")
    z, y = dev // 8, (dev // 2) % 4
    mine = jnp.concatenate(
        [
            lax.dynamic_slice(quo_bucket, (sec * QUARTER,), (QUARTER,)),
            lax.dynamic_slice(rem_bucket, (sec * QUARTER,), (QUARTER,)) + TROWS,
        ]
    )
    requests = lax.dynamic_update_slice(
        jnp.zeros((NY, 128), jnp.int32), mine[None, :], (y, z * 2 * QUARTER)
    )
    log_count = jnp.log(counts.astype(F32)).reshape(NZ, NY, 2, 2, 2, QUARTER)
    log_count = log_count.transpose(3, 2, 4, 1, 0, 5).reshape(SLOTS, 1, BLOCK)
    j = positive % 8
    core, x_hi, x_lo = (positive // 8) % 2, (positive // 16) % 2, (positive // 32) % 2
    py, pz = (positive // 64) % 4, positive // 256
    place = ((((x_hi * 2 + x_lo) * 2 + core) * NY + py) * NZ + pz) * QUARTER + j

    def vm(*shape, dtype=BF16):
        return pltpu.VMEM(shape, dtype)

    def dma(*shape):
        return pltpu.SemaphoreType.DMA(shape)

    anyspace = pl.BlockSpec(memory_space=pl.ANY)
    vmem = pl.BlockSpec(memory_space=pltpu.VMEM)
    scratch = [
        vm(TOK, DIN), vm(DIN, HID), vm(HID, DOUT), vm(4, SHARD, DIN), vm(DIN, HID), vm(HID, DOUT),
        vm(PLANE - 1, NY, 128, dtype=jnp.int32), vm(NY, 128, dtype=jnp.int32),
        vm(CHUNKS, NY, 128, WIDE), vm(CHUNKS, NY - 1, 128, WIDE),
        vm(CHUNKS, NZ, 16, WIDE), vm(CHUNKS, NZ - 1, 16, WIDE),
        vm(TOK, HID), vm(TOK, DOUT, dtype=F32), vm(TOK, DOUT),
        vm(SLOTS, NY, 64, DOUT), vm(NZ, 8, DOUT, dtype=F32), vm(NZ, 16, 512), vm(NY, 64, HID),
        vm(SLOTS, TOK, BLOCK, dtype=F32), vm(TOK, 128, dtype=F32), vm(TOK, 128, dtype=F32),
        vm(TOK, 1, dtype=F32), vm(SLOTS, TOK, BLOCK),
        vm(NX, BLOCK, DOUT), vm(NX, BLOCK, DOUT), vm(NX, BLOCK, DOUT), vm(NX - 1, BLOCK, DOUT),
        vm(NY, 64, DOUT), vm(NY - 1, 64, DOUT), vm(NZ, 8, DOUT, dtype=F32), vm(NZ - 1, 8, DOUT, dtype=F32),
        vm(NZ, 8, DOUT, dtype=F32), vm(NY, 64, DOUT),
        vm(512, DOUT, dtype=F32), vm(512, DOUT), vm(512, DOUT), vm(NX, 128, DOUT), vm(NX - 1, 128, DOUT),
        vm(512, DOUT), vm(512, DOUT), vm(NX, 128, DOUT), vm(NX - 1, 128, DOUT),
        vm(NY, 32, DOUT), vm(NY - 1, 32, DOUT), vm(NZ, 32, DOUT), vm(NY, 32, DOUT),
        vm(SLOTS, 2, 128, DOUT), vm(SLOTS, 8, 128, dtype=F32),
        dma(7),
        dma(31), dma(31), dma(2), dma(2), dma(CHUNKS, 3), dma(CHUNKS, 3), dma(CHUNKS, 7), dma(CHUNKS, 7),
        dma(7), dma(7), dma(3), dma(3), dma(3), dma(3), dma(4), dma(4),
        dma(7), dma(7), dma(3), dma(3),
        dma(4), dma(4), dma(3), dma(3), dma(3), dma(3), dma(7), dma(7),
        dma(7), dma(7), dma(3), dma(3),
        dma(1), dma(1), dma(3), dma(3),
        dma(1), dma(1), dma(3), dma(3), dma(3), dma(3), dma(7), dma(7), dma(3), dma(3),
        dma(3), dma(3), dma(4), dma(4), dma(7), dma(7),
    ]
    losses, grad_query, grad_item = pl.pallas_call(
        kernel,
        out_shape=(
            jax.ShapeDtypeStruct((TOK, 1), F32),
            jax.ShapeDtypeStruct((HID, DOUT), F32),
            jax.ShapeDtypeStruct((HID, DOUT), F32),
        ),
        in_specs=[vmem] + [anyspace] * 7 + [vmem] * 2,
        out_specs=(vmem, vmem, vmem),
        scratch_shapes=scratch,
        compiler_params=pltpu.CompilerParams(
            collective_id=0, has_side_effects=True, vmem_limit_bytes=56 * 2**20
        ),
        cost_estimate=pl.CostEstimate(flops=6_500_000_000, bytes_accessed=12_000_000, transcendentals=2_100_000),
        name="step",
    )(
        requests, user_features, w_query_in, w_query_out, quo_table, rem_table, w_item_in, w_item_out,
        log_count, place[:, None],
    )
    return (losses.reshape(TOK), grad_query, grad_item)


def solution(mesh):
    in_specs = (
        P(("sec", "dev"), None), P(), P(), P("dev", None), P("dev", None), P(), P(),
        P("dev"), P("dev"), P(), P(("sec", "dev")),
    )
    out_specs = (P(("sec", "dev")), P(), P())
    return jax.shard_map(local, mesh=mesh, in_specs=in_specs, out_specs=out_specs, check_vma=False)
```

```python
import jax
import jax.numpy as jnp
from jax import lax
from jax.experimental import pallas as pl
from jax.experimental.pallas import tpu as pltpu
from jax.sharding import PartitionSpec as P

EPS = 1e-06
INV_TEMPER = 20.0
LOG2E = 1.4426950408889634
MESH = pl.DeviceIdType.MESH
F32 = jnp.float32
BF16 = jnp.bfloat16

NX, NC, NY, NZ = 4, 2, 4, 8
PLANE = NY * NZ
TOK, DIN, HID, DOUT = 1024, 1024, 1024, 256
QUARTER = 8
BLOCK = PLANE * QUARTER
SLOTS = NX * NC
SHARD = 128
TROWS = 8192
CHUNKS = 4
WIDE = DIN // CHUNKS
TILE = 256
HALF = 128
LINE = 32
ROWS = NC * NX * LINE


def dot(a, b, ca, cb):
    return lax.dot_general(a, b, (((ca,), (cb,)), ((), ())), preferred_element_type=F32)


def norm_scale(raw):
    return lax.rsqrt(jnp.mean(raw * raw, axis=-1, keepdims=True) + EPS)


def norm_vjp(raw, grad):
    r = norm_scale(raw)
    dotted = jnp.mean(grad * raw, axis=-1, keepdims=True)
    return (grad * r - raw * (r * r * r * dotted)) * (DOUT**-0.5)


def stack(rows):
    n = rows.shape[0] // 8
    left = rows[:, :HALF].reshape(n, 8, HALF)
    right = rows[:, HALF:].reshape(n, 8, HALF)
    return jnp.concatenate([left, right], axis=1)


def unstack(tiles):
    n = tiles.shape[0]
    left = tiles[:, :8, :].reshape(n * 8, HALF)
    right = tiles[:, 8:, :].reshape(n * 8, HALF)
    return left, right


def gray(p):
    return p + jnp.where(p == 2, 1, 0) - jnp.where(p == 3, 1, 0)


def kernel(
    quo_idx, rem_idx, feat_hbm, wqi_hbm, wqo_hbm, quo_hbm, rem_hbm, wii_hbm, wio_hbm, counts_in, pos_in,
    loss_ref, fin_query, fin_item, factor_ref,
    feat, wqi, wqo, tab, wii, wio,
    idx_out, idx_recv, sel, srow, rrow, zrow, rzrow, pre,
    hq, qraw, qv, xall, gv, hz, hsrc, hcol,
    est, esum, psum, posb, invb, gall, tsrc, rc, sx, rx, town, sg, rg,
    rgv, arc, aown, asx, arx,
    qfull, qsrc, qrc, qsx, qrx, qsy, qry, qz,
    nrm, nsum, lc_ref,
    load_sem,
    idx_ss, idx_rs, tab_ss, tab_rs, ry_ss, ry_rs, rz_ss, rz_rs,
    vp_ss, vp_rs, vx_ss, vx_rs, vc_ss, vc_rs,
    hz_ss, hz_rs, hy_ss, hy_rs,
    tc_ss, tc_rs, tx_ss, tx_rs, tp_ss, tp_rs,
    gp_ss, gp_rs,
    ac_ss, ac_rs, ax_ss, ax_rs,
    qc_ss, qc_rs, qx_ss, qx_rs, qyr_ss, qyr_rs, qz_ss, qz_rs,
    f_ss, f_rs, fc_ss, fc_rs, n_ss, n_rs, ns_ss, ns_rs,
):
    sec = lax.axis_index("sec")
    dev = lax.axis_index("dev")
    xh, c = sec // 2, sec % 2
    z, y, xl = dev // 8, (dev // 2) % 4, dev % 2
    x = xh * 2 + xl
    slot = x * 2 + c
    mine = y * NZ + z
    oc = 1 - c

    def at(ax, ac, ay, az):
        return ((ax // 2) * 2 + ac, (az * NY + ay) * 2 + ax % 2)

    def zp(k):
        return at(x, c, y, (z + k) % NZ)

    def yp(k):
        return at(x, c, (y + k) % NY, z)

    def xp(k):
        return at((x + k) % NX, c, y, z)

    other = at(x, oc, y, z)
    plane = [(ky, kz) for ky in range(NY) for kz in range(NZ) if ky or kz]
    sheet = [(kx, ky) for ky in range(NY) for kx in range(NX) if kx or ky]

    def sp(kx, ky):
        return at((x + kx) % NX, c, (y + ky) % NY, z)

    def pp(i):
        ky, kz = plane[i]
        return at(x, c, (y + ky) % NY, (z + kz) % NZ)

    def pg(i):
        ky, kz = plane[i]
        return ((y + ky) % NY) * NZ + (z + kz) % NZ

    partner_x = jnp.where(c == 0, x + 1 - 2 * (x % 2), (x + 3 + 2 * (x % 2)) % NX)
    partner = at(partner_x, c, y, z)
    fin = (fin_query, fin_item)
    sent = []

    def copy(src, dst, ss, rs, target):
        return pltpu.make_async_remote_copy(
            src_ref=src, dst_ref=dst, send_sem=ss, recv_sem=rs, device_id=target, device_id_type=MESH
        )

    def push(src, dst, ss, rs, target):
        cp = copy(src, dst, ss, rs, target)
        cp.start()
        sent.append(cp)
        return cp

    barrier = pltpu.get_barrier_semaphore()
    for i in range(len(plane)):
        pl.semaphore_signal(barrier, inc=1, device_id=pp(i), device_id_type=MESH)
    greeted = len(plane) + 1
    pl.semaphore_signal(barrier, inc=1, device_id=other, device_id_type=MESH)
    for kx, ky in sheet:
        if kx:
            greeted += 1
            pl.semaphore_signal(barrier, inc=1, device_id=sp(kx, ky), device_id_type=MESH)

    loads = []
    for i, (src, dst) in enumerate(
        [
            (quo_hbm, tab.at[pl.ds(0, SHARD)]),
            (rem_hbm, tab.at[pl.ds(2 * SHARD, SHARD)]),
            (feat_hbm, feat),
            (wqi_hbm, wqi),
            (wqo_hbm, wqo),
            (wii_hbm, wii),
            (wio_hbm, wio),
        ]
    ):
        cp = pltpu.make_async_copy(src, dst, load_sem.at[i])
        cp.start()
        loads.append(cp)

    lane = lax.broadcasted_iota(jnp.int32, (NY, HALF), 1) - z * 2 * QUARTER
    lane = jnp.where(lax.broadcasted_iota(jnp.int32, (NY, HALF), 0) == y, lane, -1)
    asked = jnp.zeros((NY, HALF), jnp.int32)
    for j in range(QUARTER):
        asked = jnp.where(lane == j, quo_idx[sec * QUARTER + j], asked)
        asked = jnp.where(lane == QUARTER + j, rem_idx[sec * QUARTER + j] + TROWS, asked)
    idx_out[...] = asked
    loads[0].wait()
    loads[1].wait()
    pl.semaphore_wait(barrier, greeted)

    idx_cp = [
        push(idx_out, idx_recv.at[i], idx_ss.at[i], idx_rs.at[i], pp(i)) for i in range(len(plane))
    ]
    own_rows = pl.ds(pl.multiple_of(c * 2 * SHARD, SHARD), SHARD)
    their_rows = pl.ds(pl.multiple_of(c * 2 * SHARD + SHARD, SHARD), SHARD)
    tab_cp = push(tab.at[own_rows], tab.at[their_rows], tab_ss.at[0], tab_rs.at[0], partner)

    pos = pos_in[...]
    place = ((pos // 16) % 2) * 1024 + ((pos // 32) % 2) * 512 + ((pos // 8) % 2) * 256
    place = place + ((pos // 64) % 4) * 64 + (pos // 256) * 8 + pos % 8
    place = place.T
    for i in range(TOK // HALF):
        posb[pl.ds(i * HALF, HALF), :] = jnp.broadcast_to(place[:, i : i + 1], (HALF, HALF))

    counts = counts_in[...]
    high = (counts // 8).astype(F32).astype(BF16)
    low = (counts % 8).astype(F32).astype(BF16)
    src = lax.broadcasted_iota(jnp.int32, (HALF, BLOCK), 0)
    dst = lax.broadcasted_iota(jnp.int32, (HALF, BLOCK), 1)
    src = jnp.where((src // 64 == (dst // 64) % 2) & (src % 8 == dst % 8), (src // 8) % 8, -1)
    down = lax.broadcasted_iota(jnp.int32, (16, BLOCK), 0)
    dst = lax.broadcasted_iota(jnp.int32, (16, BLOCK), 1)
    keep = down == ((dst // 8) % 8) * 2 + dst // HALF
    for s in range(SLOTS):
        pick = (src == (s // 2 % 2) * 4 + (s // 4) * 2 + s % 2).astype(F32).astype(BF16)
        wide = dot(high, pick, 1, 0) * 8.0 + dot(low, pick, 1, 0)
        lc_ref[s] = jnp.log(jnp.sum(jnp.where(keep, wide, 0.0), axis=0, keepdims=True)) * LOG2E

    loads[2].wait()
    loads[3].wait()

    hq[...] = jnp.maximum(dot(feat[...], wqi[...], 1, 0), 0.0).astype(BF16)

    tab_cp.wait_recv()
    tabc_cp = push(tab.at[their_rows], tab.at[their_rows], tab_ss.at[1], tab_rs.at[1], other)
    for cp in idx_cp:
        cp.wait_recv()
    total = idx_out[...]
    for i in range(len(plane)):
        total = total + idx_recv[i]
    total = jnp.concatenate([total, jnp.zeros((8 - NY, HALF), jnp.int32)], axis=0).T
    line = lax.broadcasted_iota(jnp.int32, (HALF, 4 * SHARD), 1)
    which = line // SHARD
    owner = jnp.where(which % 2 == 0, dev, dev + 1 - 2 * xl)
    row_id = line % SHARD + owner * SHARD + (which // 2) * TROWS
    for i in range(NY):
        sel[i] = (row_id == total[:, i : i + 1]).astype(F32).astype(BF16)
    tabc_cp.wait_recv()

    def row_copy(ch, k):
        return copy(srow.at[ch, k], rrow.at[ch, k - 1], ry_ss.at[ch, k - 1], ry_rs.at[ch, k - 1], yp(k))

    @pl.loop(0, CHUNKS)
    def _(ch):
        cols = pl.ds(pl.multiple_of(ch * WIDE, WIDE), WIDE)
        for k in (1, 3, 2, 0):
            srow[ch, k] = dot(sel[(y + k) % NY], tab[:, cols], 1, 0).astype(BF16)
            if k:
                row_copy(ch, k).start()

    loads[4].wait()

    raw = dot(hq[...], wqo[...], 1, 0)
    qraw[...] = raw
    qv[...] = (raw * norm_scale(raw) * (DOUT**-0.5)).astype(BF16)

    def zrow_copy(ch, k):
        return copy(
            zrow.at[ch, (z + k) % NZ], rzrow.at[ch, k - 1], rz_ss.at[ch, k - 1], rz_rs.at[ch, k - 1], zp(k)
        )

    @pl.loop(0, CHUNKS)
    def _(ch):
        for k in (1, 3, 2):
            row_copy(ch, k).wait_recv()
        s = srow[ch, 0].astype(F32)
        for k in range(NY - 1):
            s = s + rrow[ch, k].astype(F32)
        zrow[ch] = s.astype(BF16).reshape(NZ, 16, WIDE)
        for k in range(1, NZ):
            zrow_copy(ch, k).start()

    loads[5].wait()
    loads[6].wait()
    pre[...] = jnp.zeros_like(pre)

    @pl.loop(0, CHUNKS)
    def _(ch):
        for k in range(1, NZ):
            zrow_copy(ch, k).wait_recv()
        s = zrow[ch, z].astype(F32)
        for k in range(NZ - 1):
            s = s + rzrow[ch, k].astype(F32)
        emb = s[:8] * s[8:]
        emb = jnp.concatenate([emb, emb], axis=0).astype(BF16)
        rows = pl.ds(pl.multiple_of(ch * WIDE, WIDE), WIDE)
        pre[...] += dot(emb, wii[rows, :], 1, 0)

    hid = jnp.maximum(pre[...], 0.0).astype(BF16)
    iraw = dot(hid, wio[...], 1, 0)[:8]
    ivec = iraw * norm_scale(iraw) * (DOUT**-0.5)
    gv[mine] = stack(ivec)[0].astype(BF16)

    v_cp = [
        push(gv.at[mine], gv.at[mine], vp_ss.at[i], vp_rs.at[i], pp(i)) for i in range(len(plane))
    ]
    hid8 = hid.astype(F32)[:8]
    hz[z] = jnp.concatenate([hid8[:, :512], hid8[:, 512:]], axis=0).astype(BF16)
    esum[...] = jnp.zeros_like(esum)
    psum[...] = jnp.zeros_like(psum)
    for cp in v_cp:
        cp.wait_recv()
    left, right = unstack(gv[...].astype(F32))
    xall[slot, :, :HALF] = left.astype(BF16)
    xall[slot, :, HALF:] = right.astype(BF16)

    def vx_copy(k):
        return copy(xall.at[slot], xall.at[slot], vx_ss.at[k - 1], vx_rs.at[k - 1], xp(k))

    for k in (1, 3, 2):
        vx_copy(k).start()
    hz_cp = [
        push(hz.at[z], hz.at[z], hz_ss.at[k - 1], hz_rs.at[k - 1], zp(k)) for k in range(1, NZ)
    ]

    def first_pass(s):
        logit = dot(qv[...], xall[s], 1, 1) * (INV_TEMPER * LOG2E) - lc_ref[s]
        e = jnp.exp2(logit)
        est[s] = e
        esum[...] += e[:, :HALF] + e[:, HALF:]
        lanes = lax.broadcasted_iota(jnp.int32, (TOK, HALF), 1)
        target = posb[...] - s * BLOCK
        hit = jnp.where(target == lanes, logit[:, :HALF], 0.0)
        hit = jnp.where(target == lanes + HALF, logit[:, HALF:], hit)
        psum[...] += hit

    def vc_copy(p):
        s = ((x + NX - gray(p)) % NX) * 2 + c
        return copy(xall.at[s], xall.at[s], vc_ss.at[p], vc_rs.at[p], other)

    @pl.loop(0, NX)
    def _(p):
        @pl.when(p > 0)
        def _():
            vx_copy(gray(p)).wait_recv()

        s = ((x + NX - gray(p)) % NX) * 2
        vc_copy(p).start()
        first_pass(s + c)
        vc_copy(p).wait_recv()
        first_pass(s + oc)

    for cp in hz_cp:
        cp.wait_recv()
    hv = hz[...].astype(F32)
    hv = jnp.concatenate([hv[:, :8, :].reshape(64, 512), hv[:, 8:, :].reshape(64, 512)], axis=1)
    hv = hv.astype(BF16)
    for i in range(NY):
        hsrc[i] = hv[:, i * ROWS : (i + 1) * ROWS]
    hcol[y] = hsrc[y]
    hy_cp = [
        push(hsrc.at[(y + k) % NY], hcol.at[y], hy_ss.at[k - 1], hy_rs.at[k - 1], yp(k))
        for k in range(1, NY)
    ]
    sums = jnp.sum(esum[...], axis=1, keepdims=True)
    picked = jnp.sum(psum[...], axis=1, keepdims=True)
    invb[...] = jnp.broadcast_to(1.0 / sums, (TOK, HALF))
    loss = (jnp.log2(sums) - picked) * (1.0 / LOG2E)
    loss = jnp.broadcast_to(loss, (TOK, HALF)).reshape(TOK // HALF, HALF, HALF)
    down = lax.broadcasted_iota(jnp.int32, (TOK // HALF, HALF, HALF), 1)
    across = lax.broadcasted_iota(jnp.int32, (TOK // HALF, HALF, HALF), 2)
    loss_ref[...] = jnp.sum(jnp.where(down == across, loss, 0.0), axis=1)

    def weigh(s):
        lanes = lax.broadcasted_iota(jnp.int32, (TOK, HALF), 1)
        target = posb[...] - s * BLOCK
        scale = invb[...]
        pa = est[s, :, :HALF] * scale
        pb = est[s, :, HALF:] * scale
        gall[s, :, :HALF] = jnp.where(target == lanes, pa - 1.0, pa).astype(BF16)
        gall[s, :, HALF:] = jnp.where(target == lanes + HALF, pb - 1.0, pb).astype(BF16)

    def spread(s):
        return dot(gall[s], qv[...], 0, 0) * INV_TEMPER

    def tc_copy(k):
        return copy(tsrc.at[k], rc.at[k], tc_ss.at[k], tc_rs.at[k], other)

    def tx_copy(k):
        return copy(sx.at[k], rx.at[k - 1], tx_ss.at[k - 1], tx_rs.at[k - 1], xp(k))

    @pl.loop(0, NX)
    def _(p):
        k = gray((p + 1) % NX)
        s = ((x + k) % NX) * 2
        weigh(s + oc)
        weigh(s + c)
        tsrc[k] = spread(s + oc).astype(BF16)
        tc_copy(k).start()
        t = spread(s + c)
        tc_copy(k).wait_recv()
        t = t + rc[k].astype(F32)
        sx[k] = t.astype(BF16)

        @pl.when(p < NX - 1)
        def _():
            tx_copy(k).start()

        @pl.when(p == NX - 1)
        def _():
            town[...] = t

    acc = dot(gall[0], xall[0], 1, 0)
    for s in range(1, SLOTS):
        acc = acc + dot(gall[s], xall[s], 1, 0)
    qv[...] = norm_vjp(qraw[...], acc * INV_TEMPER).astype(BF16)

    qfull[...] = dot(hq[...], qv[...], 0, 0)

    def core_rows(i, core):
        return pl.ds(pl.multiple_of(i * ROWS + core * HALF, HALF), HALF)

    for i in range(NY):
        qsrc[i] = qfull[core_rows(i, oc), :].astype(BF16)
    qc_cp = push(qsrc, qrc, qc_ss.at[0], qc_rs.at[0], other)

    for k in (1, 3, 2):
        tx_copy(k).wait_recv()
    t = town[...]
    for k in range(NX - 1):
        t = t + rx[k].astype(F32)
    sg[...] = stack(t).astype(BF16)
    tp_cp = [push(sg.at[pg(i)], rg.at[i], tp_ss.at[i], tp_rs.at[i], pp(i)) for i in range(len(plane))]

    qc_cp.wait_recv()
    for i in range(NY):
        q = qfull[core_rows(i, c), :] + qrc[i].astype(F32)
        qsx[:, i] = q.reshape(NX, LINE, DOUT).astype(BF16)
    qx_cp = [
        push(qsx.at[(x + k) % NX], qrx.at[k - 1], qx_ss.at[k - 1], qx_rs.at[k - 1], xp(k))
        for k in (1, 3, 2)
    ]

    for cp in tp_cp:
        cp.wait_recv()
    t = sg[mine].astype(F32)
    for i in range(len(plane)):
        t = t + rg[i].astype(F32)
    t = jnp.concatenate([t[:8], t[8:]], axis=1)
    rgv[mine] = stack(norm_vjp(iraw, t))[0].astype(BF16)
    gp_cp = [push(rgv.at[mine], rgv.at[mine], gp_ss.at[i], gp_rs.at[i], pp(i)) for i in range(len(plane))]

    for cp in qx_cp:
        cp.wait_recv()
    q = qsx[x].astype(F32)
    for k in range(NX - 1):
        q = q + qrx[k].astype(F32)
    qsy[...] = q.astype(BF16)
    qy_cp = [
        push(qsy.at[(y + k) % NY], qry.at[k - 1], qyr_ss.at[k - 1], qyr_rs.at[k - 1], yp(k))
        for k in range(1, NY)
    ]

    for cp in qy_cp:
        cp.wait_recv()
    q = qsy[y].astype(F32)
    for k in range(NY - 1):
        q = q + qry[k].astype(F32)
    qz[z] = q.astype(BF16)
    qz_cp = [
        push(qz.at[z], qz.at[z], qz_ss.at[k - 1], qz_rs.at[k - 1], zp(k)) for k in range(1, NZ)
    ]

    for cp in hy_cp:
        cp.wait_recv()
    for cp in gp_cp:
        cp.wait_recv()
    left, right = unstack(rgv[...].astype(F32))
    raw_grad = jnp.concatenate([left, right], axis=1).astype(BF16)
    aown[...] = dot(hcol[...].reshape(BLOCK, ROWS), raw_grad, 0, 0)
    ac_cp = push(aown.at[core_rows(0, oc)], arc, ac_ss.at[0], ac_rs.at[0], other)

    ac_cp.wait_recv()
    asx[...] = (aown[core_rows(0, c), :] + arc[...]).reshape(NX, LINE, DOUT)
    ax_cp = [
        push(asx.at[(x + k) % NX], arx.at[k - 1], ax_ss.at[k - 1], ax_rs.at[k - 1], xp(k))
        for k in (1, 3, 2)
    ]

    def square_sum(v):
        v = jnp.sum(v * v, axis=0, keepdims=True)
        return v[:, :HALF] + v[:, HALF:]

    def gather(m):
        return [
            push(fin[m].at[y, c, x], fin[m].at[y, c, x], f_ss.at[m, i], f_rs.at[m, i], sp(kx, ky))
            for i, (kx, ky) in enumerate(sheet)
        ]

    for cp in qz_cp:
        cp.wait_recv()
    q = qz[0].astype(F32)
    for k in range(1, NZ):
        q = q + qz[k].astype(F32)
    fin_query[y, c, x] = q.astype(BF16)
    qf_cp = gather(0)

    for cp in ax_cp:
        cp.wait_recv()
    a = asx[x]
    for k in range(NX - 1):
        a = a + arx[k]
    fin_item[y, c, x] = a.astype(BF16)
    af_cp = gather(1)
    nrm[y, x] = square_sum(q) + square_sum(a)
    n_cp = [
        push(nrm.at[y, x], nrm.at[y, x], n_ss.at[i], n_rs.at[i], sp(kx, ky))
        for i, (kx, ky) in enumerate(sheet)
    ]
    fc_cp = []
    for m, cps in ((0, qf_cp), (1, af_cp)):
        for ky in range(NY):
            for cp, (_, k) in zip(cps, sheet):
                if k == ky:
                    cp.wait_recv()
            block = fin[m].at[(y + NY - ky) % NY, c]
            fc_cp.append(push(block, block, fc_ss.at[m, ky], fc_rs.at[m, ky], other))
    for cp in n_cp:
        cp.wait_recv()
    square = jnp.sum(nrm[...].reshape(NX * NY, HALF), axis=0, keepdims=True)
    nsum[0] = square
    ns_cp = push(nsum.at[0], nsum.at[1], ns_ss.at[0], ns_rs.at[0], other)
    ns_cp.wait_recv()
    norm = jnp.sqrt(jnp.sum(square + nsum[1], axis=1, keepdims=True))
    limit = (HID * DOUT / 2) ** 0.5
    factor_ref[...] = jnp.broadcast_to(limit / jnp.maximum(norm, limit), (1, DOUT))
    for cp in fc_cp:
        cp.wait_recv()
    for cp in sent:
        cp.wait_send()
    for k in range(1, NX):
        vx_copy(k).wait_send()
        tx_copy(k).wait_send()
    for k in range(NX):
        vc_copy(k).wait_send()
        tc_copy(k).wait_send()

    @pl.loop(0, CHUNKS)
    def _(ch):
        for k in range(1, NY):
            row_copy(ch, k).wait_send()
        for k in range(1, NZ):
            zrow_copy(ch, k).wait_send()


def local(
    user_features, w_query_in, w_query_out, quo_table, rem_table, w_item_in, w_item_out,
    quo_bucket, rem_bucket, counts, positive,
):
    def vm(*shape, dtype=BF16):
        return pltpu.VMEM(shape, dtype)

    def dma(*shape):
        return [pltpu.SemaphoreType.DMA(shape)] * 2

    anyspace = pl.BlockSpec(memory_space=pl.ANY)
    vmem = pl.BlockSpec(memory_space=pltpu.VMEM)
    smem = pl.BlockSpec(memory_space=pltpu.SMEM)
    scratch = [
        vm(TOK, DIN), vm(DIN, HID), vm(HID, DOUT), vm(4 * SHARD, DIN), vm(DIN, HID), vm(HID, DOUT),
        vm(NY, HALF, dtype=jnp.int32), vm(PLANE - 1, NY, HALF, dtype=jnp.int32), vm(NY, HALF, 4 * SHARD),
        vm(CHUNKS, NY, HALF, WIDE), vm(CHUNKS, NY - 1, HALF, WIDE),
        vm(CHUNKS, NZ, 16, WIDE), vm(CHUNKS, NZ - 1, 16, WIDE), vm(16, HID, dtype=F32),
        vm(TOK, HID), vm(TOK, DOUT, dtype=F32), vm(TOK, DOUT),
        vm(SLOTS, BLOCK, DOUT), vm(PLANE, 16, HALF), vm(NZ, 16, 512), vm(NY, 64, ROWS), vm(NY, 64, ROWS),
        vm(SLOTS, TOK, BLOCK, dtype=F32), vm(TOK, HALF, dtype=F32), vm(TOK, HALF, dtype=F32),
        vm(TOK, HALF, dtype=jnp.int32), vm(TOK, HALF, dtype=F32), vm(SLOTS, TOK, BLOCK),
        vm(NX, BLOCK, DOUT), vm(NX, BLOCK, DOUT), vm(NX, BLOCK, DOUT), vm(NX - 1, BLOCK, DOUT),
        vm(BLOCK, DOUT, dtype=F32), vm(PLANE, 16, HALF), vm(PLANE - 1, 16, HALF),
        vm(PLANE, 16, HALF), vm(HALF, DOUT, dtype=F32), vm(ROWS, DOUT, dtype=F32),
        vm(NX, LINE, DOUT, dtype=F32), vm(NX - 1, LINE, DOUT, dtype=F32),
        vm(HID, DOUT, dtype=F32), vm(NY, HALF, DOUT), vm(NY, HALF, DOUT),
        vm(NX, NY, LINE, DOUT), vm(NX - 1, NY, LINE, DOUT), vm(NY, LINE, DOUT), vm(NY - 1, LINE, DOUT),
        vm(NZ, LINE, DOUT),
        vm(NY, NX, 1, HALF, dtype=F32), vm(2, 1, HALF, dtype=F32), vm(SLOTS, 1, BLOCK, dtype=F32),
        pltpu.SemaphoreType.DMA((7,)),
        *dma(31), *dma(2), *dma(CHUNKS, 3), *dma(CHUNKS, 7),
        *dma(31), *dma(3), *dma(4),
        *dma(7), *dma(3),
        *dma(4), *dma(3), *dma(31),
        *dma(31),
        *dma(1), *dma(3),
        *dma(1), *dma(3), *dma(3), *dma(7),
        *dma(2, 15), *dma(2, 4), *dma(15), *dma(1),
    ]
    losses, grad_query, grad_item, factor = pl.pallas_call(
        kernel,
        out_shape=(
            jax.ShapeDtypeStruct((TOK // HALF, HALF), F32),
            jax.ShapeDtypeStruct((NY, NC, NX, LINE, DOUT), BF16),
            jax.ShapeDtypeStruct((NY, NC, NX, LINE, DOUT), BF16),
            jax.ShapeDtypeStruct((1, DOUT), F32),
        ),
        in_specs=[smem] * 2 + [anyspace] * 7 + [vmem] * 2,
        out_specs=(vmem, vmem, vmem, vmem),
        scratch_shapes=scratch,
        compiler_params=pltpu.CompilerParams(
            collective_id=0, has_side_effects=True, vmem_limit_bytes=56 * 2**20
        ),
        cost_estimate=pl.CostEstimate(flops=6_500_000_000, bytes_accessed=12_000_000, transcendentals=2_100_000),
        name="step",
    )(
        quo_bucket, rem_bucket, user_features, w_query_in, w_query_out, quo_table, rem_table, w_item_in,
        w_item_out, counts.reshape(16, HALF), positive.reshape(TOK // HALF, HALF),
    )
    def scaled(grad):
        return grad.reshape(HID, DOUT).astype(F32) * factor

    return (losses.reshape(TOK), scaled(grad_query), scaled(grad_item))


def solution(mesh):
    in_specs = (
        P(("sec", "dev"), None), P(), P(), P("dev", None), P("dev", None), P(), P(),
        P("dev"), P("dev"), P(), P(("sec", "dev")),
    )
    out_specs = (P(("sec", "dev")), P(), P())
    return jax.shard_map(local, mesh=mesh, in_specs=in_specs, out_specs=out_specs, check_vma=False)
```

```python
import jax
import jax.numpy as jnp
from jax import lax
from jax.experimental import pallas as pl
from jax.experimental.pallas import tpu as pltpu
from jax.sharding import PartitionSpec as P

EPS = 1e-06
INV_TEMPER = 20.0
LOG2E = 1.4426950408889634
MESH = pl.DeviceIdType.MESH
F32 = jnp.float32
BF16 = jnp.bfloat16

NX, NC, NY, NZ = 4, 2, 4, 8
PLANE = NY * NZ
TOK, DIN, HID, DOUT = 1024, 1024, 1024, 256
QUARTER = 8
BLOCK = PLANE * QUARTER
SLOTS = NX * NC
SHARD = 128
TROWS = 8192
CHUNKS = 4
ORDER = (0, 1, 2, 3)
WIDE = DIN // CHUNKS
TILE = 256
HALF = 128
LINE = 32
ROWS = NC * NX * LINE


def dot(a, b, ca, cb):
    return lax.dot_general(a, b, (((ca,), (cb,)), ((), ())), preferred_element_type=F32)


def norm_scale(raw):
    return lax.rsqrt(jnp.mean(raw * raw, axis=-1, keepdims=True) + EPS)


def norm_vjp(raw, grad):
    r = norm_scale(raw)
    dotted = jnp.mean(grad * raw, axis=-1, keepdims=True)
    return (grad * r - raw * (r * r * r * dotted)) * (DOUT**-0.5)


def stack(rows):
    n = rows.shape[0] // 8
    left = rows[:, :HALF].reshape(n, 8, HALF)
    right = rows[:, HALF:].reshape(n, 8, HALF)
    return jnp.concatenate([left, right], axis=1)


def unstack(tiles):
    n = tiles.shape[0]
    left = tiles[:, :8, :].reshape(n * 8, HALF)
    right = tiles[:, 8:, :].reshape(n * 8, HALF)
    return left, right


def gray(p):
    return p + jnp.where(p == 2, 1, 0) - jnp.where(p == 3, 1, 0)


def kernel(
    quo_idx, rem_idx, feat_hbm, wqi_hbm, wqo_hbm, quo_hbm, rem_hbm, wii_hbm, wio_hbm, counts_in, pos_in,
    loss_ref, fin_query, fin_item, factor_ref,
    feat, wqi, wqo, tab, wii, wio,
    idx_out, idx_recv, sel, srow, rrow, zrow, rzrow, pre,
    hq, qraw, qv, xall, gv, hz, hsrc, hcol,
    est, esum, psum, posb, invb, gall, tsrc, rc, sx, rx, town, sg, rg,
    rgv, arc, aown, asx, arx,
    qfull, qsrc, qrc, qsx, qrx, qsy, qry, qz,
    nrm, nsum, lc_ref,
    load_sem,
    idx_ss, idx_rs, tab_ss, tab_rs, ry_ss, ry_rs, rz_ss, rz_rs,
    vp_ss, vp_rs, vx_ss, vx_rs, vc_ss, vc_rs,
    hz_ss, hz_rs, hy_ss, hy_rs,
    tc_ss, tc_rs, tx_ss, tx_rs, tp_ss, tp_rs,
    gp_ss, gp_rs,
    ac_ss, ac_rs, ax_ss, ax_rs,
    qc_ss, qc_rs, qx_ss, qx_rs, qy_ss, qy_rs, qz_ss, qz_rs,
    f_ss, f_rs, fc_ss, fc_rs, n_ss, n_rs, ns_ss, ns_rs,
):
    sec = lax.axis_index("sec")
    dev = lax.axis_index("dev")
    xh, c = sec // 2, sec % 2
    z, y, xl = dev // 8, (dev // 2) % 4, dev % 2
    x = xh * 2 + xl
    slot = x * 2 + c
    mine = y * NZ + z
    oc = 1 - c

    def at(ax, ac, ay, az):
        return ((ax // 2) * 2 + ac, (az * NY + ay) * 2 + ax % 2)

    def zp(k):
        return at(x, c, y, (z + k) % NZ)

    def yp(k):
        return at(x, c, (y + k) % NY, z)

    def xp(k):
        return at((x + k) % NX, c, y, z)

    other = at(x, oc, y, z)
    plane = [(ky, kz) for ky in range(NY) for kz in range(NZ) if ky or kz]
    sheet = [(kx, ky) for ky in range(NY) for kx in range(NX) if kx or ky]

    def sp(kx, ky):
        return at((x + kx) % NX, c, (y + ky) % NY, z)

    def pp(i):
        ky, kz = plane[i]
        return at(x, c, (y + ky) % NY, (z + kz) % NZ)

    def pg(i):
        ky, kz = plane[i]
        return ((y + ky) % NY) * NZ + (z + kz) % NZ

    partner_x = jnp.where(c == 0, x + 1 - 2 * (x % 2), (x + 3 + 2 * (x % 2)) % NX)
    partner = at(partner_x, c, y, z)
    fin = (fin_query, fin_item)
    sent = []

    def copy(src, dst, ss, rs, target):
        return pltpu.make_async_remote_copy(
            src_ref=src, dst_ref=dst, send_sem=ss, recv_sem=rs, device_id=target, device_id_type=MESH
        )

    def push(src, dst, ss, rs, target):
        cp = copy(src, dst, ss, rs, target)
        cp.start()
        sent.append(cp)
        return cp

    def landed(region, rs):
        copy(region, region, rs, rs, other).wait_recv()

    def left_here(region, ss):
        sent.append(copy(region, region, ss, ss, other))

    def flush():
        for cp in sent:
            cp.wait_send()
        sent.clear()

    barrier = pltpu.get_barrier_semaphore()
    for i in range(len(plane)):
        pl.semaphore_signal(barrier, inc=1, device_id=pp(i), device_id_type=MESH)
    greeted = len(plane) + 1
    pl.semaphore_signal(barrier, inc=1, device_id=other, device_id_type=MESH)
    for kx, ky in sheet:
        if kx:
            greeted += 1
            pl.semaphore_signal(barrier, inc=1, device_id=sp(kx, ky), device_id_type=MESH)

    loads = []

    def load(src, dst):
        cp = pltpu.make_async_copy(src, dst, load_sem.at[len(loads)])
        cp.start()
        loads.append(cp)

    for ch in range(CHUNKS):
        load(quo_hbm.at[:, ch * WIDE : (ch + 1) * WIDE], tab.at[ch, pl.ds(0, SHARD)])
        load(rem_hbm.at[:, ch * WIDE : (ch + 1) * WIDE], tab.at[ch, pl.ds(2 * SHARD, SHARD)])
    for src, dst in ((feat_hbm, feat), (wqi_hbm, wqi), (wqo_hbm, wqo), (wii_hbm, wii), (wio_hbm, wio)):
        load(src, dst)

    lane = lax.broadcasted_iota(jnp.int32, (NY, HALF), 1) - z * 2 * QUARTER
    lane = jnp.where(lax.broadcasted_iota(jnp.int32, (NY, HALF), 0) == y, lane, -1)
    asked = jnp.zeros((NY, HALF), jnp.int32)
    for j in range(QUARTER):
        asked = jnp.where(lane == j, quo_idx[sec * QUARTER + j], asked)
        asked = jnp.where(lane == QUARTER + j, rem_idx[sec * QUARTER + j] + TROWS, asked)
    idx_out[...] = asked
    for i in range(2 * CHUNKS):
        loads[i].wait()
    pl.semaphore_wait(barrier, greeted)

    for i in range(len(plane)):
        copy(idx_out, idx_recv.at[i], idx_ss.at[0], idx_rs.at[0], pp(i)).start()
    left_here(idx_recv, idx_ss.at[0])
    own_rows = pl.ds(pl.multiple_of(c * 2 * SHARD, SHARD), SHARD)
    their_rows = pl.ds(pl.multiple_of(c * 2 * SHARD + SHARD, SHARD), SHARD)

    def tab_copy(ch):
        return copy(
            tab.at[ch, own_rows], tab.at[ch, their_rows], tab_ss.at[0, ch], tab_rs.at[0, ch], partner
        )

    def tab_core_copy(ch):
        return copy(
            tab.at[ch, their_rows], tab.at[ch, their_rows], tab_ss.at[1, ch], tab_rs.at[1, ch], other
        )

    for ch in ORDER:
        tab_copy(ch).start()

    pos = pos_in[...]
    place = ((pos // 16) % 2) * 1024 + ((pos // 32) % 2) * 512 + ((pos // 8) % 2) * 256
    place = place + ((pos // 64) % 4) * 64 + (pos // 256) * 8 + pos % 8
    place = place.T
    for i in range(TOK // HALF):
        posb[pl.ds(i * HALF, HALF), :] = jnp.broadcast_to(place[:, i : i + 1], (HALF, HALF))

    counts = counts_in[...]
    high = (counts // 8).astype(F32).astype(BF16)
    low = (counts % 8).astype(F32).astype(BF16)
    src = lax.broadcasted_iota(jnp.int32, (HALF, BLOCK), 0)
    dst = lax.broadcasted_iota(jnp.int32, (HALF, BLOCK), 1)
    src = jnp.where((src // 64 == (dst // 64) % 2) & (src % 8 == dst % 8), (src // 8) % 8, -1)
    down = lax.broadcasted_iota(jnp.int32, (16, BLOCK), 0)
    dst = lax.broadcasted_iota(jnp.int32, (16, BLOCK), 1)
    keep = down == ((dst // 8) % 8) * 2 + dst // HALF
    for s in range(SLOTS):
        pick = (src == (s // 2 % 2) * 4 + (s // 4) * 2 + s % 2).astype(F32).astype(BF16)
        wide = dot(high, pick, 1, 0) * 8.0 + dot(low, pick, 1, 0)
        lc_ref[s] = jnp.log(jnp.sum(jnp.where(keep, wide, 0.0), axis=0, keepdims=True)) * LOG2E

    loads[2 * CHUNKS].wait()
    loads[2 * CHUNKS + 1].wait()

    hq[...] = jnp.maximum(dot(feat[...], wqi[...], 1, 0), 0.0).astype(BF16)

    tab_copy(ORDER[0]).wait_recv()
    tab_core_copy(ORDER[0]).start()
    landed(idx_recv, idx_rs.at[0])
    total = idx_out[...]
    for i in range(len(plane)):
        total = total + idx_recv[i]
    total = jnp.concatenate([total, jnp.zeros((8 - NY, HALF), jnp.int32)], axis=0).T
    line = lax.broadcasted_iota(jnp.int32, (HALF, 4 * SHARD), 1)
    which = line // SHARD
    owner = jnp.where(which % 2 == 0, dev, dev + 1 - 2 * xl)
    row_id = line % SHARD + owner * SHARD + (which // 2) * TROWS
    for i in range(NY):
        sel[i] = (row_id == total[:, i : i + 1]).astype(F32).astype(BF16)

    def row_copy(ch, k):
        return copy(srow.at[ch, k], rrow.at[ch, k - 1], ry_ss.at[ch], ry_rs.at[ch], yp(k))

    for i, ch in enumerate(ORDER):
        if i < CHUNKS - 1:
            tab_copy(ORDER[i + 1]).wait_recv()
            tab_core_copy(ORDER[i + 1]).start()
        tab_core_copy(ch).wait_recv()
        for k in (1, 3, 2, 0):
            srow[ch, k] = dot(sel[(y + k) % NY], tab[ch], 1, 0).astype(BF16)
            if k:
                row_copy(ch, k).start()
        left_here(rrow.at[ch], ry_ss.at[ch])
        sent.append(tab_copy(ch))
        sent.append(tab_core_copy(ch))

    loads[2 * CHUNKS + 2].wait()

    raw = dot(hq[...], wqo[...], 1, 0)
    qraw[...] = raw
    qv[...] = (raw * norm_scale(raw) * (DOUT**-0.5)).astype(BF16)

    def zrow_copy(ch, k):
        return copy(
            zrow.at[ch, (z + k) % NZ], rzrow.at[ch, k - 1], rz_ss.at[ch], rz_rs.at[ch], zp(k)
        )

    for ch in ORDER:
        landed(rrow.at[ch], ry_rs.at[ch])
        s = srow[ch, 0].astype(F32)
        for k in range(NY - 1):
            s = s + rrow[ch, k].astype(F32)
        zrow[ch] = s.astype(BF16).reshape(NZ, 16, WIDE)
        for k in range(1, NZ):
            zrow_copy(ch, k).start()
    flush()
    for ch in ORDER:
        left_here(rzrow.at[ch], rz_ss.at[ch])

    loads[2 * CHUNKS + 3].wait()
    loads[2 * CHUNKS + 4].wait()
    pre[...] = jnp.zeros_like(pre)

    for ch in ORDER:
        landed(rzrow.at[ch], rz_rs.at[ch])
        s = zrow[ch, z].astype(F32)
        for k in range(NZ - 1):
            s = s + rzrow[ch, k].astype(F32)
        emb = s[:8] * s[8:]
        emb = jnp.concatenate([emb, emb], axis=0).astype(BF16)
        pre[...] += dot(emb, wii[ch * WIDE : (ch + 1) * WIDE, :], 1, 0)

    hid = jnp.maximum(pre[...], 0.0).astype(BF16)
    iraw = dot(hid, wio[...], 1, 0)[:8]
    ivec = iraw * norm_scale(iraw) * (DOUT**-0.5)
    gv[mine] = stack(ivec)[0].astype(BF16)

    for i in range(len(plane)):
        copy(gv.at[mine], gv.at[mine], vp_ss.at[0], vp_rs.at[0], pp(i)).start()
    flush()
    left_here(gv.at[pl.ds(0, PLANE - 1)], vp_ss.at[0])
    hid8 = hid.astype(F32)[:8]
    hz[z] = jnp.concatenate([hid8[:, :512], hid8[:, 512:]], axis=0).astype(BF16)
    esum[...] = jnp.zeros_like(esum)
    psum[...] = jnp.zeros_like(psum)
    landed(gv.at[pl.ds(0, PLANE - 1)], vp_rs.at[0])
    left, right = unstack(gv[...].astype(F32))
    xall[slot, :, :HALF] = left.astype(BF16)
    xall[slot, :, HALF:] = right.astype(BF16)

    def vx_copy(k):
        return copy(xall.at[slot], xall.at[slot], vx_ss.at[k - 1], vx_rs.at[k - 1], xp(k))

    for k in (1, 3, 2):
        vx_copy(k).start()
    for k in range(1, NZ):
        copy(hz.at[z], hz.at[z], hz_ss.at[0], hz_rs.at[0], zp(k)).start()
    left_here(hz.at[pl.ds(0, NZ - 1)], hz_ss.at[0])

    def first_pass(s):
        logit = dot(qv[...], xall[s], 1, 1) * (INV_TEMPER * LOG2E) - lc_ref[s]
        e = jnp.exp2(logit)
        est[s] = e
        esum[...] += e[:, :HALF] + e[:, HALF:]
        lanes = lax.broadcasted_iota(jnp.int32, (TOK, HALF), 1)
        target = posb[...] - s * BLOCK
        hit = jnp.where(target == lanes, logit[:, :HALF], 0.0)
        hit = jnp.where(target == lanes + HALF, logit[:, HALF:], hit)
        psum[...] += hit

    def vc_copy(p):
        s = ((x + NX - gray(p)) % NX) * 2 + c
        return copy(xall.at[s], xall.at[s], vc_ss.at[p], vc_rs.at[p], other)

    @pl.loop(0, NX)
    def _(p):
        @pl.when(p > 0)
        def _():
            vx_copy(gray(p)).wait_recv()

        s = ((x + NX - gray(p)) % NX) * 2
        vc_copy(p).start()
        first_pass(s + c)
        vc_copy(p).wait_recv()
        first_pass(s + oc)

    landed(hz.at[pl.ds(0, NZ - 1)], hz_rs.at[0])
    hv = hz[...].astype(F32)
    hv = jnp.concatenate([hv[:, :8, :].reshape(64, 512), hv[:, 8:, :].reshape(64, 512)], axis=1)
    hv = hv.astype(BF16)
    for i in range(NY):
        hsrc[i] = hv[:, i * ROWS : (i + 1) * ROWS]
    hcol[y] = hsrc[y]
    for k in range(1, NY):
        copy(hsrc.at[(y + k) % NY], hcol.at[y], hy_ss.at[0], hy_rs.at[0], yp(k)).start()
    left_here(hcol.at[pl.ds(0, NY - 1)], hy_ss.at[0])
    sums = jnp.sum(esum[...], axis=1, keepdims=True)
    picked = jnp.sum(psum[...], axis=1, keepdims=True)
    invb[...] = jnp.broadcast_to(1.0 / sums, (TOK, HALF))
    loss = (jnp.log2(sums) - picked) * (1.0 / LOG2E)
    loss = jnp.broadcast_to(loss, (TOK, HALF)).reshape(TOK // HALF, HALF, HALF)
    down = lax.broadcasted_iota(jnp.int32, (TOK // HALF, HALF, HALF), 1)
    across = lax.broadcasted_iota(jnp.int32, (TOK // HALF, HALF, HALF), 2)
    loss_ref[...] = jnp.sum(jnp.where(down == across, loss, 0.0), axis=1)

    def weigh(s):
        lanes = lax.broadcasted_iota(jnp.int32, (TOK, HALF), 1)
        target = posb[...] - s * BLOCK
        scale = invb[...]
        pa = est[s, :, :HALF] * scale
        pb = est[s, :, HALF:] * scale
        gall[s, :, :HALF] = jnp.where(target == lanes, pa - 1.0, pa).astype(BF16)
        gall[s, :, HALF:] = jnp.where(target == lanes + HALF, pb - 1.0, pb).astype(BF16)

    def spread(s):
        return dot(gall[s], qv[...], 0, 0) * INV_TEMPER

    def tc_copy(k):
        return copy(tsrc.at[k], rc.at[k], tc_ss.at[k], tc_rs.at[k], other)

    def tx_copy(k):
        return copy(sx.at[k], rx.at[k - 1], tx_ss.at[0], tx_rs.at[0], xp(k))

    @pl.loop(0, NX)
    def _(p):
        k = gray((p + 1) % NX)
        s = ((x + k) % NX) * 2
        weigh(s + oc)
        weigh(s + c)
        tsrc[k] = spread(s + oc).astype(BF16)
        tc_copy(k).start()
        t = spread(s + c)
        tc_copy(k).wait_recv()
        t = t + rc[k].astype(F32)
        sx[k] = t.astype(BF16)

        @pl.when(p < NX - 1)
        def _():
            tx_copy(k).start()

        @pl.when(p == NX - 1)
        def _():
            town[...] = t

    acc = dot(gall[0], xall[0], 1, 0)
    for s in range(1, SLOTS):
        acc = acc + dot(gall[s], xall[s], 1, 0)
    qv[...] = norm_vjp(qraw[...], acc * INV_TEMPER).astype(BF16)

    qfull[...] = dot(hq[...], qv[...], 0, 0)

    def core_rows(i, core):
        return pl.ds(pl.multiple_of(i * ROWS + core * HALF, HALF), HALF)

    for i in range(NY):
        qsrc[i] = qfull[core_rows(i, oc), :].astype(BF16)
    qc_cp = push(qsrc, qrc, qc_ss.at[0], qc_rs.at[0], other)

    flush()
    for k in range(1, NX):
        sent.append(vx_copy(k))
    for k in range(NX):
        sent.append(vc_copy(k))
        sent.append(tc_copy(k))
    left_here(rx, tx_ss.at[0])
    landed(rx, tx_rs.at[0])
    t = town[...]
    for k in range(NX - 1):
        t = t + rx[k].astype(F32)
    sg[...] = stack(t).astype(BF16)
    for i in range(len(plane)):
        copy(sg.at[pg(i)], rg.at[i], tp_ss.at[0], tp_rs.at[0], pp(i)).start()

    qc_cp.wait_recv()
    for i in range(NY):
        q = qfull[core_rows(i, c), :] + qrc[i].astype(F32)
        qsx[:, i] = q.reshape(NX, LINE, DOUT).astype(BF16)
    for k in (1, 3, 2):
        copy(qsx.at[(x + k) % NX], qrx.at[k - 1], qx_ss.at[0], qx_rs.at[0], xp(k)).start()
    flush()
    left_here(rg, tp_ss.at[0])
    left_here(qrx, qx_ss.at[0])

    landed(rg, tp_rs.at[0])
    t = sg[mine].astype(F32)
    for i in range(len(plane)):
        t = t + rg[i].astype(F32)
    t = jnp.concatenate([t[:8], t[8:]], axis=1)
    rgv[mine] = stack(norm_vjp(iraw, t))[0].astype(BF16)
    for i in range(len(plane)):
        copy(rgv.at[mine], rgv.at[mine], gp_ss.at[0], gp_rs.at[0], pp(i)).start()

    landed(qrx, qx_rs.at[0])
    q = qsx[x].astype(F32)
    for k in range(NX - 1):
        q = q + qrx[k].astype(F32)
    qsy[...] = q.astype(BF16)
    for k in range(1, NY):
        copy(qsy.at[(y + k) % NY], qry.at[k - 1], qy_ss.at[0], qy_rs.at[0], yp(k)).start()
    flush()
    left_here(rgv.at[pl.ds(0, PLANE - 1)], gp_ss.at[0])
    left_here(qry, qy_ss.at[0])

    landed(qry, qy_rs.at[0])
    q = qsy[y].astype(F32)
    for k in range(NY - 1):
        q = q + qry[k].astype(F32)
    qz[z] = q.astype(BF16)
    for k in range(1, NZ):
        copy(qz.at[z], qz.at[z], qz_ss.at[0], qz_rs.at[0], zp(k)).start()
    left_here(qz.at[pl.ds(0, NZ - 1)], qz_ss.at[0])

    landed(hcol.at[pl.ds(0, NY - 1)], hy_rs.at[0])
    landed(rgv.at[pl.ds(0, PLANE - 1)], gp_rs.at[0])
    left, right = unstack(rgv[...].astype(F32))
    raw_grad = jnp.concatenate([left, right], axis=1).astype(BF16)
    aown[...] = dot(hcol[...].reshape(BLOCK, ROWS), raw_grad, 0, 0)
    ac_cp = push(aown.at[core_rows(0, oc)], arc, ac_ss.at[0], ac_rs.at[0], other)

    ac_cp.wait_recv()
    asx[...] = (aown[core_rows(0, c), :] + arc[...]).reshape(NX, LINE, DOUT)
    for k in (1, 3, 2):
        copy(asx.at[(x + k) % NX], arx.at[k - 1], ax_ss.at[0], ax_rs.at[0], xp(k)).start()
    flush()
    left_here(arx, ax_ss.at[0])

    def square_sum(v):
        v = jnp.sum(v * v, axis=0, keepdims=True)
        return v[:, :HALF] + v[:, HALF:]

    def group(ref, ky, lead):
        return ref.at[lead + (pl.ds(0, NX - 1),)] if ky == 0 else ref.at[lead]

    def gather(m):
        for kx, ky in sheet:
            copy(
                fin[m].at[y, c, x], fin[m].at[y, c, x], f_ss.at[m, ky], f_rs.at[m, ky], sp(kx, ky)
            ).start()
        for ky in range(NY):
            left_here(group(fin[m], ky, (0, 0)), f_ss.at[m, ky])

    def gather_core(m):
        for ky in range(NY):
            landed(group(fin[m], ky, (0, 0)), f_rs.at[m, ky])
            block = fin[m].at[(y + NY - ky) % NY, c]
            fc_cp.append(push(block, block, fc_ss.at[m, ky], fc_rs.at[m, ky], other))

    fc_cp = []

    landed(qz.at[pl.ds(0, NZ - 1)], qz_rs.at[0])
    q = qz[0].astype(F32)
    for k in range(1, NZ):
        q = q + qz[k].astype(F32)
    fin_query[y, c, x] = q.astype(BF16)
    gather(0)

    landed(arx, ax_rs.at[0])
    a = asx[x]
    for k in range(NX - 1):
        a = a + arx[k]
    fin_item[y, c, x] = a.astype(BF16)
    gather(1)
    nrm[y, x] = square_sum(q) + square_sum(a)
    for kx, ky in sheet:
        copy(nrm.at[y, x], nrm.at[y, x], n_ss.at[ky], n_rs.at[ky], sp(kx, ky)).start()
    gather_core(0)
    flush()
    gather_core(1)
    for ky in range(NY):
        left_here(group(nrm, ky, (0,)), n_ss.at[ky])
        landed(group(nrm, ky, (0,)), n_rs.at[ky])
    square = jnp.sum(nrm[...].reshape(NX * NY, HALF), axis=0, keepdims=True)
    nsum[0] = square
    ns_cp = push(nsum.at[0], nsum.at[1], ns_ss.at[0], ns_rs.at[0], other)
    ns_cp.wait_recv()
    norm = jnp.sqrt(jnp.sum(square + nsum[1], axis=1, keepdims=True))
    limit = (HID * DOUT / 2) ** 0.5
    factor_ref[...] = jnp.broadcast_to(limit / jnp.maximum(norm, limit), (1, DOUT))
    for cp in fc_cp:
        cp.wait_recv()
    flush()


def local(
    user_features, w_query_in, w_query_out, quo_table, rem_table, w_item_in, w_item_out,
    quo_bucket, rem_bucket, counts, positive,
):
    def vm(*shape, dtype=BF16):
        return pltpu.VMEM(shape, dtype)

    def dma(*shape):
        return [pltpu.SemaphoreType.DMA(shape)] * 2

    anyspace = pl.BlockSpec(memory_space=pl.ANY)
    vmem = pl.BlockSpec(memory_space=pltpu.VMEM)
    smem = pl.BlockSpec(memory_space=pltpu.SMEM)
    scratch = [
        vm(TOK, DIN), vm(DIN, HID), vm(HID, DOUT), vm(CHUNKS, 4 * SHARD, WIDE), vm(DIN, HID), vm(HID, DOUT),
        vm(NY, HALF, dtype=jnp.int32), vm(PLANE - 1, NY, HALF, dtype=jnp.int32), vm(NY, HALF, 4 * SHARD),
        vm(CHUNKS, NY, HALF, WIDE), vm(CHUNKS, NY - 1, HALF, WIDE),
        vm(CHUNKS, NZ, 16, WIDE), vm(CHUNKS, NZ - 1, 16, WIDE), vm(16, HID, dtype=F32),
        vm(TOK, HID), vm(TOK, DOUT, dtype=F32), vm(TOK, DOUT),
        vm(SLOTS, BLOCK, DOUT), vm(PLANE, 16, HALF), vm(NZ, 16, 512), vm(NY, 64, ROWS), vm(NY, 64, ROWS),
        vm(SLOTS, TOK, BLOCK, dtype=F32), vm(TOK, HALF, dtype=F32), vm(TOK, HALF, dtype=F32),
        vm(TOK, HALF, dtype=jnp.int32), vm(TOK, HALF, dtype=F32), vm(SLOTS, TOK, BLOCK),
        vm(NX, BLOCK, DOUT), vm(NX, BLOCK, DOUT), vm(NX, BLOCK, DOUT), vm(NX - 1, BLOCK, DOUT),
        vm(BLOCK, DOUT, dtype=F32), vm(PLANE, 16, HALF), vm(PLANE - 1, 16, HALF),
        vm(PLANE, 16, HALF), vm(HALF, DOUT, dtype=F32), vm(ROWS, DOUT, dtype=F32),
        vm(NX, LINE, DOUT, dtype=F32), vm(NX - 1, LINE, DOUT, dtype=F32),
        vm(HID, DOUT, dtype=F32), vm(NY, HALF, DOUT), vm(NY, HALF, DOUT),
        vm(NX, NY, LINE, DOUT), vm(NX - 1, NY, LINE, DOUT), vm(NY, LINE, DOUT), vm(NY - 1, LINE, DOUT),
        vm(NZ, LINE, DOUT),
        vm(NY, NX, 1, HALF, dtype=F32), vm(2, 1, HALF, dtype=F32), vm(SLOTS, 1, BLOCK, dtype=F32),
        pltpu.SemaphoreType.DMA((2 * CHUNKS + 5,)),
        *dma(1), *dma(2, CHUNKS), *dma(CHUNKS), *dma(CHUNKS),
        *dma(1), *dma(3), *dma(4),
        *dma(1), *dma(1),
        *dma(4), *dma(1), *dma(1),
        *dma(1),
        *dma(1), *dma(1),
        *dma(1), *dma(1), *dma(1), *dma(1),
        *dma(2, 4), *dma(2, 4), *dma(4), *dma(1),
    ]
    losses, grad_query, grad_item, factor = pl.pallas_call(
        kernel,
        out_shape=(
            jax.ShapeDtypeStruct((TOK // HALF, HALF), F32),
            jax.ShapeDtypeStruct((NY, NC, NX, LINE, DOUT), BF16),
            jax.ShapeDtypeStruct((NY, NC, NX, LINE, DOUT), BF16),
            jax.ShapeDtypeStruct((1, DOUT), F32),
        ),
        in_specs=[smem] * 2 + [anyspace] * 7 + [vmem] * 2,
        out_specs=(vmem, vmem, vmem, vmem),
        scratch_shapes=scratch,
        compiler_params=pltpu.CompilerParams(
            collective_id=0, has_side_effects=True, vmem_limit_bytes=56 * 2**20
        ),
        cost_estimate=pl.CostEstimate(flops=6_500_000_000, bytes_accessed=12_000_000, transcendentals=2_100_000),
        name="step",
    )(
        quo_bucket, rem_bucket, user_features, w_query_in, w_query_out, quo_table, rem_table, w_item_in,
        w_item_out, counts.reshape(16, HALF), positive.reshape(TOK // HALF, HALF),
    )
    def scaled(grad):
        return grad.reshape(HID, DOUT).astype(F32) * factor

    return (losses.reshape(TOK), scaled(grad_query), scaled(grad_item))


def solution(mesh):
    in_specs = (
        P(("sec", "dev"), None), P(), P(), P("dev", None), P("dev", None), P(), P(),
        P("dev"), P("dev"), P(), P(("sec", "dev")),
    )
    out_specs = (P(("sec", "dev")), P(), P())
    return jax.shard_map(local, mesh=mesh, in_specs=in_specs, out_specs=out_specs, check_vma=False)
```

```python
import jax
import jax.numpy as jnp
from jax import lax
from jax.experimental import pallas as pl
from jax.experimental.pallas import tpu as pltpu
from jax.sharding import PartitionSpec as P

EPS = 1e-06
INV_TEMPER = 20.0
LOG2E = 1.4426950408889634
MESH = pl.DeviceIdType.MESH
F32 = jnp.float32
BF16 = jnp.bfloat16

NX, NC, NY, NZ = 4, 2, 4, 8
PLANE = NY * NZ
TOK, DIN, HID, DOUT = 1024, 1024, 1024, 256
QUARTER = 8
BLOCK = PLANE * QUARTER
SLOTS = NX * NC
SHARD = 128
TROWS = 8192
CHUNKS = 4
ZFIRST = 3
ORDER = (0, ZFIRST, 1, 2)


def hops(k, n):
    return min(k, n - k)


Z_FAR = sorted(range(1, NZ), key=lambda k: -hops(k, NZ))
WIDE = DIN // CHUNKS
TILE = 256
HALF = 128
LINE = 32
ROWS = NC * NX * LINE


def dot(a, b, ca, cb):
    return lax.dot_general(a, b, (((ca,), (cb,)), ((), ())), preferred_element_type=F32)


def norm_scale(raw):
    return lax.rsqrt(jnp.mean(raw * raw, axis=-1, keepdims=True) + EPS)


def norm_vjp(raw, grad):
    r = norm_scale(raw)
    dotted = jnp.mean(grad * raw, axis=-1, keepdims=True)
    return (grad * r - raw * (r * r * r * dotted)) * (DOUT**-0.5)


def stack(rows):
    n = rows.shape[0] // 8
    left = rows[:, :HALF].reshape(n, 8, HALF)
    right = rows[:, HALF:].reshape(n, 8, HALF)
    return jnp.concatenate([left, right], axis=1)


def unstack(tiles):
    n = tiles.shape[0]
    left = tiles[:, :8, :].reshape(n * 8, HALF)
    right = tiles[:, 8:, :].reshape(n * 8, HALF)
    return left, right


GRAY = (0, 1, 3, 2)


def kernel(
    quo_idx, rem_idx, feat_hbm, wqi_hbm, wqo_hbm, quo_hbm, rem_hbm, wii_hbm, wio_hbm, counts_in, pos_in,
    loss_ref, fin_query, fin_item, factor_ref,
    feat, wqi, wqo, tab, wii, wio,
    idx_out, idx_recv, sel, srow, rrow, zrow, rzrow, srz, rrz, sry, rry, pre,
    hq, qraw, qv, xall, gv, hz, hsrc, hcol,
    est, esum, psum, posb, invb, gall, tsrc, rc, sx, rx, town, sg, rg,
    rgv, arc, aown, asx, arx,
    qfull, qsrc, qrc, qsx, qrx, qsy, qry, qz,
    nrm, nsum, lc_ref,
    load_sem,
    idx_ss, idx_rs, tab_ss, tab_rs, ry_ss, ry_rs, rz_ss, rz_rs, rf_ss, rf_rs, rl_ss, rl_rs,
    vp_ss, vp_rs, vx_ss, vx_rs, vc_ss, vc_rs,
    hz_ss, hz_rs, hy_ss, hy_rs,
    tc_ss, tc_rs, tx_ss, tx_rs, tp_ss, tp_rs,
    gp_ss, gp_rs,
    ac_ss, ac_rs, ax_ss, ax_rs,
    qc_ss, qc_rs, qx_ss, qx_rs, qy_ss, qy_rs, qz_ss, qz_rs,
    f_ss, f_rs, fc_ss, fc_rs, n_ss, n_rs, ns_ss, ns_rs,
):
    sec = lax.axis_index("sec")
    dev = lax.axis_index("dev")
    xh, c = sec // 2, sec % 2
    z, y, xl = dev // 8, (dev // 2) % 4, dev % 2
    x = xh * 2 + xl
    slot = x * 2 + c
    mine = y * NZ + z
    oc = 1 - c

    def at(ax, ac, ay, az):
        return ((ax // 2) * 2 + ac, (az * NY + ay) * 2 + ax % 2)

    def zp(k):
        return at(x, c, y, (z + k) % NZ)

    def yp(k):
        return at(x, c, (y + k) % NY, z)

    def xp(k):
        return at((x + k) % NX, c, y, z)

    other = at(x, oc, y, z)
    plane = [(ky, kz) for ky in range(NY) for kz in range(NZ) if ky or kz]
    plane.sort(key=lambda p: -hops(p[0], NY) - hops(p[1], NZ))
    sheet = [(kx, ky) for ky in range(NY) for kx in range(NX) if kx or ky]
    sheet.sort(key=lambda p: -hops(p[0], NX) - hops(p[1], NY))

    def sp(kx, ky):
        return at((x + kx) % NX, c, (y + ky) % NY, z)

    def pp(i):
        ky, kz = plane[i]
        return at(x, c, (y + ky) % NY, (z + kz) % NZ)

    def pg(i):
        ky, kz = plane[i]
        return ((y + ky) % NY) * NZ + (z + kz) % NZ

    partner_x = jnp.where(c == 0, x + 1 - 2 * (x % 2), (x + 3 + 2 * (x % 2)) % NX)
    partner = at(partner_x, c, y, z)
    fin = (fin_query, fin_item)
    sent = []

    def copy(src, dst, ss, rs, target):
        return pltpu.make_async_remote_copy(
            src_ref=src, dst_ref=dst, send_sem=ss, recv_sem=rs, device_id=target, device_id_type=MESH
        )

    def push(src, dst, ss, rs, target):
        cp = copy(src, dst, ss, rs, target)
        cp.start()
        sent.append(cp)
        return cp

    def landed(region, rs):
        copy(region, region, rs, rs, other).wait_recv()

    def left_here(region, ss):
        sent.append(copy(region, region, ss, ss, other))

    def flush():
        for cp in sent:
            cp.wait_send()
        sent.clear()

    barrier = pltpu.get_barrier_semaphore()
    for i in range(len(plane)):
        pl.semaphore_signal(barrier, inc=1, device_id=pp(i), device_id_type=MESH)
    greeted = len(plane) + 1
    pl.semaphore_signal(barrier, inc=1, device_id=other, device_id_type=MESH)
    for kx, ky in sheet:
        if kx:
            greeted += 1
            pl.semaphore_signal(barrier, inc=1, device_id=sp(kx, ky), device_id_type=MESH)

    loads = []

    def load(src, dst):
        cp = pltpu.make_async_copy(src, dst, load_sem.at[len(loads)])
        cp.start()
        loads.append(cp)

    for ch in range(CHUNKS):
        load(quo_hbm.at[:, ch * WIDE : (ch + 1) * WIDE], tab.at[ch, pl.ds(0, SHARD)])
        load(rem_hbm.at[:, ch * WIDE : (ch + 1) * WIDE], tab.at[ch, pl.ds(2 * SHARD, SHARD)])
    for src, dst in ((feat_hbm, feat), (wqi_hbm, wqi), (wqo_hbm, wqo), (wii_hbm, wii), (wio_hbm, wio)):
        load(src, dst)

    lane = lax.broadcasted_iota(jnp.int32, (NY, HALF), 1) - z * 2 * QUARTER
    lane = jnp.where(lax.broadcasted_iota(jnp.int32, (NY, HALF), 0) == y, lane, -1)
    asked = jnp.zeros((NY, HALF), jnp.int32)
    for j in range(QUARTER):
        asked = jnp.where(lane == j, quo_idx[sec * QUARTER + j], asked)
        asked = jnp.where(lane == QUARTER + j, rem_idx[sec * QUARTER + j] + TROWS, asked)
    idx_out[...] = asked
    for i in range(2 * CHUNKS):
        loads[i].wait()
    pl.semaphore_wait(barrier, greeted)

    for i in range(len(plane)):
        copy(idx_out, idx_recv.at[i], idx_ss.at[0], idx_rs.at[0], pp(i)).start()
    left_here(idx_recv, idx_ss.at[0])
    own_rows = pl.ds(pl.multiple_of(c * 2 * SHARD, SHARD), SHARD)
    their_rows = pl.ds(pl.multiple_of(c * 2 * SHARD + SHARD, SHARD), SHARD)

    def tab_copy(ch):
        return copy(
            tab.at[ch, own_rows], tab.at[ch, their_rows], tab_ss.at[0, ch], tab_rs.at[0, ch], partner
        )

    def tab_core_copy(ch):
        return copy(
            tab.at[ch, their_rows], tab.at[ch, their_rows], tab_ss.at[1, ch], tab_rs.at[1, ch], other
        )

    for ch in ORDER:
        tab_copy(ch).start()

    pos = pos_in[...]
    place = ((pos // 16) % 2) * 1024 + ((pos // 32) % 2) * 512 + ((pos // 8) % 2) * 256
    place = place + ((pos // 64) % 4) * 64 + (pos // 256) * 8 + pos % 8
    place = place.T
    for i in range(TOK // HALF):
        posb[pl.ds(i * HALF, HALF), :] = jnp.broadcast_to(place[:, i : i + 1], (HALF, HALF))

    counts = counts_in[...]
    high = (counts // 8).astype(F32).astype(BF16)
    low = (counts % 8).astype(F32).astype(BF16)
    src = lax.broadcasted_iota(jnp.int32, (HALF, BLOCK), 0)
    dst = lax.broadcasted_iota(jnp.int32, (HALF, BLOCK), 1)
    src = jnp.where((src // 64 == (dst // 64) % 2) & (src % 8 == dst % 8), (src // 8) % 8, -1)
    down = lax.broadcasted_iota(jnp.int32, (16, BLOCK), 0)
    dst = lax.broadcasted_iota(jnp.int32, (16, BLOCK), 1)
    keep = down == ((dst // 8) % 8) * 2 + dst // HALF
    for s in range(SLOTS):
        pick = (src == (s // 2 % 2) * 4 + (s // 4) * 2 + s % 2).astype(F32).astype(BF16)
        wide = dot(high, pick, 1, 0) * 8.0 + dot(low, pick, 1, 0)
        lc_ref[s] = jnp.log(jnp.sum(jnp.where(keep, wide, 0.0), axis=0, keepdims=True)) * LOG2E

    loads[2 * CHUNKS].wait()
    loads[2 * CHUNKS + 1].wait()

    hq[...] = jnp.maximum(dot(feat[...], wqi[...], 1, 0), 0.0).astype(BF16)

    tab_copy(ORDER[0]).wait_recv()
    tab_core_copy(ORDER[0]).start()
    landed(idx_recv, idx_rs.at[0])
    total = idx_out[...]
    for i in range(len(plane)):
        total = total + idx_recv[i]
    total = jnp.concatenate([total, jnp.zeros((8 - NY, HALF), jnp.int32)], axis=0).T
    line = lax.broadcasted_iota(jnp.int32, (HALF, 4 * SHARD), 1)
    which = line // SHARD
    owner = jnp.where(which % 2 == 0, dev, dev + 1 - 2 * xl)
    row_id = line % SHARD + owner * SHARD + (which // 2) * TROWS
    for i in range(NY):
        sel[i] = (row_id == total[:, i : i + 1]).astype(F32).astype(BF16)

    def row_copy(ch, k):
        return copy(srow.at[ch, k], rrow.at[ch, k - 1], ry_ss.at[ch], ry_rs.at[ch], yp(k))

    for i, ch in enumerate(ORDER):
        if i < CHUNKS - 1:
            tab_copy(ORDER[i + 1]).wait_recv()
            tab_core_copy(ORDER[i + 1]).start()
        tab_core_copy(ch).wait_recv()
        if ch == ZFIRST:
            for i in range(NY):
                got = dot(sel[i], tab[ch], 1, 0).astype(BF16)
                srz[:, i * 16 : (i + 1) * 16, :] = got.reshape(NZ, 16, WIDE)
            for k in Z_FAR:
                copy(srz.at[(z + k) % NZ], rrz.at[k - 1], rf_ss.at[0], rf_rs.at[0], zp(k)).start()
            left_here(rrz, rf_ss.at[0])
        else:
            for k in (2, 1, 3, 0):
                srow[ch, k] = dot(sel[(y + k) % NY], tab[ch], 1, 0).astype(BF16)
                if k:
                    row_copy(ch, k).start()
            left_here(rrow.at[ch], ry_ss.at[ch])
        sent.append(tab_copy(ch))
        sent.append(tab_core_copy(ch))

    loads[2 * CHUNKS + 2].wait()

    raw = dot(hq[...], wqo[...], 1, 0)
    qraw[...] = raw
    qv[...] = (raw * norm_scale(raw) * (DOUT**-0.5)).astype(BF16)

    def zrow_copy(ch, k):
        return copy(
            zrow.at[ch, (z + k) % NZ], rzrow.at[ch, k - 1], rz_ss.at[ch], rz_rs.at[ch], zp(k)
        )

    def along_z(ch):
        landed(rrow.at[ch], ry_rs.at[ch])
        s = srow[ch, 0].astype(F32)
        for k in range(NY - 1):
            s = s + rrow[ch, k].astype(F32)
        zrow[ch] = s.astype(BF16).reshape(NZ, 16, WIDE)
        for k in Z_FAR:
            zrow_copy(ch, k).start()
        left_here(rzrow.at[ch], rz_ss.at[ch])

    along_z(0)
    along_z(1)
    landed(rrz, rf_rs.at[0])
    s = srz[z].astype(F32)
    for k in range(NZ - 1):
        s = s + rrz[k].astype(F32)
    sry[...] = s.astype(BF16).reshape(NY, 16, WIDE)
    for k in (2, 1, 3):
        copy(sry.at[(y + k) % NY], rry.at[k - 1], rl_ss.at[0], rl_rs.at[0], yp(k)).start()
    left_here(rry, rl_ss.at[0])
    along_z(2)

    loads[2 * CHUNKS + 3].wait()
    loads[2 * CHUNKS + 4].wait()
    pre[...] = jnp.zeros_like(pre)

    for ch in (0, 1, ZFIRST, 2):
        if ch == ZFIRST:
            landed(rry, rl_rs.at[0])
            s = sry[y].astype(F32)
            for k in range(NY - 1):
                s = s + rry[k].astype(F32)
        else:
            landed(rzrow.at[ch], rz_rs.at[ch])
            s = zrow[ch, z].astype(F32)
            for k in range(NZ - 1):
                s = s + rzrow[ch, k].astype(F32)
        emb = s[:8] * s[8:]
        emb = jnp.concatenate([emb, emb], axis=0).astype(BF16)
        pre[...] += dot(emb, wii[ch * WIDE : (ch + 1) * WIDE, :], 1, 0)

    hid = jnp.maximum(pre[...], 0.0).astype(BF16)
    iraw = dot(hid, wio[...], 1, 0)[:8]
    ivec = iraw * norm_scale(iraw) * (DOUT**-0.5)
    gv[mine] = stack(ivec)[0].astype(BF16)

    for i in range(len(plane)):
        copy(gv.at[mine], gv.at[mine], vp_ss.at[0], vp_rs.at[0], pp(i)).start()
    flush()
    left_here(gv.at[pl.ds(0, PLANE - 1)], vp_ss.at[0])
    hid8 = hid.astype(F32)[:8]
    hz[z] = jnp.concatenate([hid8[:, :512], hid8[:, 512:]], axis=0).astype(BF16)
    esum[...] = jnp.zeros_like(esum)
    psum[...] = jnp.zeros_like(psum)
    landed(gv.at[pl.ds(0, PLANE - 1)], vp_rs.at[0])
    left, right = unstack(gv[...].astype(F32))
    xall[slot, :, :HALF] = left.astype(BF16)
    xall[slot, :, HALF:] = right.astype(BF16)

    def vx_copy(k):
        return copy(xall.at[slot], xall.at[slot], vx_ss.at[k - 1], vx_rs.at[k - 1], xp(k))

    for k in (1, 3, 2):
        vx_copy(k).start()
    for k in Z_FAR:
        copy(hz.at[z], hz.at[z], hz_ss.at[0], hz_rs.at[0], zp(k)).start()
    left_here(hz.at[pl.ds(0, NZ - 1)], hz_ss.at[0])

    def first_pass(s):
        logit = dot(qv[...], xall[s], 1, 1) * (INV_TEMPER * LOG2E) - lc_ref[s]
        e = jnp.exp2(logit)
        est[s] = e
        esum[...] += e[:, :HALF] + e[:, HALF:]
        lanes = lax.broadcasted_iota(jnp.int32, (TOK, HALF), 1)
        target = posb[...] - s * BLOCK
        hit = jnp.where(target == lanes, logit[:, :HALF], 0.0)
        hit = jnp.where(target == lanes + HALF, logit[:, HALF:], hit)
        psum[...] += hit

    def vc_copy(p):
        s = ((x + NX - GRAY[p]) % NX) * 2 + c
        return copy(xall.at[s], xall.at[s], vc_ss.at[p], vc_rs.at[p], other)

    for p in range(NX):
        if p:
            vx_copy(GRAY[p]).wait_recv()
        s = ((x + NX - GRAY[p]) % NX) * 2
        vc_copy(p).start()
        first_pass(s + c)
        vc_copy(p).wait_recv()
        first_pass(s + oc)

    landed(hz.at[pl.ds(0, NZ - 1)], hz_rs.at[0])
    hv = hz[...].astype(F32)
    hv = jnp.concatenate([hv[:, :8, :].reshape(64, 512), hv[:, 8:, :].reshape(64, 512)], axis=1)
    hv = hv.astype(BF16)
    for i in range(NY):
        hsrc[i] = hv[:, i * ROWS : (i + 1) * ROWS]
    hcol[y] = hsrc[y]
    for k in range(1, NY):
        copy(hsrc.at[(y + k) % NY], hcol.at[y], hy_ss.at[0], hy_rs.at[0], yp(k)).start()
    left_here(hcol.at[pl.ds(0, NY - 1)], hy_ss.at[0])
    sums = jnp.sum(esum[...], axis=1, keepdims=True)
    picked = jnp.sum(psum[...], axis=1, keepdims=True)
    invb[...] = jnp.broadcast_to(1.0 / sums, (TOK, HALF))
    loss = (jnp.log2(sums) - picked) * (1.0 / LOG2E)
    loss = jnp.broadcast_to(loss, (TOK, HALF)).reshape(TOK // HALF, HALF, HALF)
    down = lax.broadcasted_iota(jnp.int32, (TOK // HALF, HALF, HALF), 1)
    across = lax.broadcasted_iota(jnp.int32, (TOK // HALF, HALF, HALF), 2)
    loss_ref[...] = jnp.sum(jnp.where(down == across, loss, 0.0), axis=1)

    def weigh(s):
        lanes = lax.broadcasted_iota(jnp.int32, (TOK, HALF), 1)
        target = posb[...] - s * BLOCK
        scale = invb[...]
        pa = est[s, :, :HALF] * scale
        pb = est[s, :, HALF:] * scale
        gall[s, :, :HALF] = jnp.where(target == lanes, pa - 1.0, pa).astype(BF16)
        gall[s, :, HALF:] = jnp.where(target == lanes + HALF, pb - 1.0, pb).astype(BF16)

    def spread(s):
        return dot(gall[s], qv[...], 0, 0) * INV_TEMPER

    def tc_copy(k):
        return copy(tsrc.at[k], rc.at[k], tc_ss.at[k], tc_rs.at[k], other)

    def tx_copy(k):
        return copy(sx.at[k], rx.at[k - 1], tx_ss.at[0], tx_rs.at[0], xp(k))

    def settle(k):
        tc_copy(k).wait_recv()
        t = town[k] + rc[k].astype(F32)
        if k:
            sx[k] = t.astype(BF16)
            tx_copy(k).start()
        else:
            town[k] = t

    for p in range(NX):
        k = GRAY[(p + 1) % NX]
        s = ((x + k) % NX) * 2
        weigh(s + oc)
        weigh(s + c)
        tsrc[k] = spread(s + oc).astype(BF16)
        tc_copy(k).start()
        if p:
            settle(GRAY[p])
        town[k] = spread(s + c)
    settle(0)

    acc = dot(gall[0], xall[0], 1, 0)
    for s in range(1, SLOTS):
        acc = acc + dot(gall[s], xall[s], 1, 0)
    qv[...] = norm_vjp(qraw[...], acc * INV_TEMPER).astype(BF16)

    qfull[...] = dot(hq[...], qv[...], 0, 0)

    def core_rows(i, core):
        return pl.ds(pl.multiple_of(i * ROWS + core * HALF, HALF), HALF)

    for i in range(NY):
        qsrc[i] = qfull[core_rows(i, oc), :].astype(BF16)
    qc_cp = push(qsrc, qrc, qc_ss.at[0], qc_rs.at[0], other)

    flush()
    for k in range(1, NX):
        sent.append(vx_copy(k))
    for k in range(NX):
        sent.append(vc_copy(k))
        sent.append(tc_copy(k))
    left_here(rx, tx_ss.at[0])
    landed(rx, tx_rs.at[0])
    t = town[0]
    for k in range(NX - 1):
        t = t + rx[k].astype(F32)
    sg[...] = stack(t).astype(BF16)
    for i in range(len(plane)):
        copy(sg.at[pg(i)], rg.at[i], tp_ss.at[0], tp_rs.at[0], pp(i)).start()

    qc_cp.wait_recv()
    for i in range(NY):
        q = qfull[core_rows(i, c), :] + qrc[i].astype(F32)
        qsx[:, i] = q.reshape(NX, LINE, DOUT).astype(BF16)
    for k in (1, 3, 2):
        copy(qsx.at[(x + k) % NX], qrx.at[k - 1], qx_ss.at[0], qx_rs.at[0], xp(k)).start()
    flush()
    left_here(rg, tp_ss.at[0])
    left_here(qrx, qx_ss.at[0])

    landed(rg, tp_rs.at[0])
    t = sg[mine].astype(F32)
    for i in range(len(plane)):
        t = t + rg[i].astype(F32)
    t = jnp.concatenate([t[:8], t[8:]], axis=1)
    rgv[mine] = stack(norm_vjp(iraw, t))[0].astype(BF16)
    for i in range(len(plane)):
        copy(rgv.at[mine], rgv.at[mine], gp_ss.at[0], gp_rs.at[0], pp(i)).start()

    landed(qrx, qx_rs.at[0])
    q = qsx[x].astype(F32)
    for k in range(NX - 1):
        q = q + qrx[k].astype(F32)
    qsy[...] = q.astype(BF16)
    for k in range(1, NY):
        copy(qsy.at[(y + k) % NY], qry.at[k - 1], qy_ss.at[0], qy_rs.at[0], yp(k)).start()
    flush()
    left_here(rgv.at[pl.ds(0, PLANE - 1)], gp_ss.at[0])
    left_here(qry, qy_ss.at[0])

    landed(qry, qy_rs.at[0])
    q = qsy[y].astype(F32)
    for k in range(NY - 1):
        q = q + qry[k].astype(F32)
    qz[z] = q.astype(BF16)
    for k in Z_FAR:
        copy(qz.at[z], qz.at[z], qz_ss.at[0], qz_rs.at[0], zp(k)).start()
    left_here(qz.at[pl.ds(0, NZ - 1)], qz_ss.at[0])

    landed(hcol.at[pl.ds(0, NY - 1)], hy_rs.at[0])
    landed(rgv.at[pl.ds(0, PLANE - 1)], gp_rs.at[0])
    left, right = unstack(rgv[...].astype(F32))
    raw_grad = jnp.concatenate([left, right], axis=1).astype(BF16)
    aown[...] = dot(hcol[...].reshape(BLOCK, ROWS), raw_grad, 0, 0)
    ac_cp = push(aown.at[core_rows(0, oc)], arc, ac_ss.at[0], ac_rs.at[0], other)

    ac_cp.wait_recv()
    asx[...] = (aown[core_rows(0, c), :] + arc[...]).reshape(NX, LINE, DOUT)
    for k in (2, 1, 3):
        copy(asx.at[(x + k) % NX], arx.at[k - 1], ax_ss.at[0], ax_rs.at[0], xp(k)).start()
    flush()
    left_here(arx, ax_ss.at[0])

    def square_sum(v):
        v = jnp.sum(v * v, axis=0, keepdims=True)
        return v[:, :HALF] + v[:, HALF:]

    def group(ref, ky, lead):
        return ref.at[lead + (pl.ds(0, NX - 1),)] if ky == 0 else ref.at[lead]

    def gather(m):
        for kx, ky in sheet:
            copy(
                fin[m].at[y, c, x], fin[m].at[y, c, x], f_ss.at[m, ky], f_rs.at[m, ky], sp(kx, ky)
            ).start()
        for ky in range(NY):
            left_here(group(fin[m], ky, (0, 0)), f_ss.at[m, ky])

    def gather_core(m):
        for ky in range(NY):
            landed(group(fin[m], ky, (0, 0)), f_rs.at[m, ky])
            block = fin[m].at[(y + NY - ky) % NY, c]
            fc_cp.append(push(block, block, fc_ss.at[m, ky], fc_rs.at[m, ky], other))

    fc_cp = []

    landed(qz.at[pl.ds(0, NZ - 1)], qz_rs.at[0])
    q = qz[0].astype(F32)
    for k in range(1, NZ):
        q = q + qz[k].astype(F32)
    fin_query[y, c, x] = q.astype(BF16)
    gather(0)

    landed(arx, ax_rs.at[0])
    a = asx[x]
    for k in range(NX - 1):
        a = a + arx[k]
    fin_item[y, c, x] = a.astype(BF16)
    gather(1)
    nrm[y, x] = square_sum(q) + square_sum(a)
    for kx, ky in sheet:
        copy(nrm.at[y, x], nrm.at[y, x], n_ss.at[ky], n_rs.at[ky], sp(kx, ky)).start()
    gather_core(0)
    flush()
    gather_core(1)
    for ky in range(NY):
        left_here(group(nrm, ky, (0,)), n_ss.at[ky])
        landed(group(nrm, ky, (0,)), n_rs.at[ky])
    square = jnp.sum(nrm[...].reshape(NX * NY, HALF), axis=0, keepdims=True)
    nsum[0] = square
    ns_cp = push(nsum.at[0], nsum.at[1], ns_ss.at[0], ns_rs.at[0], other)
    ns_cp.wait_recv()
    norm = jnp.sqrt(jnp.sum(square + nsum[1], axis=1, keepdims=True))
    limit = (HID * DOUT / 2) ** 0.5
    factor_ref[...] = jnp.broadcast_to(limit / jnp.maximum(norm, limit), (1, DOUT))
    for cp in fc_cp:
        cp.wait_recv()
    flush()


def local(
    user_features, w_query_in, w_query_out, quo_table, rem_table, w_item_in, w_item_out,
    quo_bucket, rem_bucket, counts, positive,
):
    def vm(*shape, dtype=BF16):
        return pltpu.VMEM(shape, dtype)

    def dma(*shape):
        return [pltpu.SemaphoreType.DMA(shape)] * 2

    anyspace = pl.BlockSpec(memory_space=pl.ANY)
    vmem = pl.BlockSpec(memory_space=pltpu.VMEM)
    smem = pl.BlockSpec(memory_space=pltpu.SMEM)
    scratch = [
        vm(TOK, DIN), vm(DIN, HID), vm(HID, DOUT), vm(CHUNKS, 4 * SHARD, WIDE), vm(DIN, HID), vm(HID, DOUT),
        vm(NY, HALF, dtype=jnp.int32), vm(PLANE - 1, NY, HALF, dtype=jnp.int32), vm(NY, HALF, 4 * SHARD),
        vm(CHUNKS - 1, NY, HALF, WIDE), vm(CHUNKS - 1, NY - 1, HALF, WIDE),
        vm(CHUNKS - 1, NZ, 16, WIDE), vm(CHUNKS - 1, NZ - 1, 16, WIDE),
        vm(NZ, NY * 16, WIDE), vm(NZ - 1, NY * 16, WIDE), vm(NY, 16, WIDE), vm(NY - 1, 16, WIDE),
        vm(16, HID, dtype=F32),
        vm(TOK, HID), vm(TOK, DOUT, dtype=F32), vm(TOK, DOUT),
        vm(SLOTS, BLOCK, DOUT), vm(PLANE, 16, HALF), vm(NZ, 16, 512), vm(NY, 64, ROWS), vm(NY, 64, ROWS),
        vm(SLOTS, TOK, BLOCK, dtype=F32), vm(TOK, HALF, dtype=F32), vm(TOK, HALF, dtype=F32),
        vm(TOK, HALF, dtype=jnp.int32), vm(TOK, HALF, dtype=F32), vm(SLOTS, TOK, BLOCK),
        vm(NX, BLOCK, DOUT), vm(NX, BLOCK, DOUT), vm(NX, BLOCK, DOUT), vm(NX - 1, BLOCK, DOUT),
        vm(NX, BLOCK, DOUT, dtype=F32), vm(PLANE, 16, HALF), vm(PLANE - 1, 16, HALF),
        vm(PLANE, 16, HALF), vm(HALF, DOUT, dtype=F32), vm(ROWS, DOUT, dtype=F32),
        vm(NX, LINE, DOUT, dtype=F32), vm(NX - 1, LINE, DOUT, dtype=F32),
        vm(HID, DOUT, dtype=F32), vm(NY, HALF, DOUT), vm(NY, HALF, DOUT),
        vm(NX, NY, LINE, DOUT), vm(NX - 1, NY, LINE, DOUT), vm(NY, LINE, DOUT), vm(NY - 1, LINE, DOUT),
        vm(NZ, LINE, DOUT),
        vm(NY, NX, 1, HALF, dtype=F32), vm(2, 1, HALF, dtype=F32), vm(SLOTS, 1, BLOCK, dtype=F32),
        pltpu.SemaphoreType.DMA((2 * CHUNKS + 5,)),
        *dma(1), *dma(2, CHUNKS), *dma(CHUNKS - 1), *dma(CHUNKS - 1), *dma(1), *dma(1),
        *dma(1), *dma(3), *dma(4),
        *dma(1), *dma(1),
        *dma(4), *dma(1), *dma(1),
        *dma(1),
        *dma(1), *dma(1),
        *dma(1), *dma(1), *dma(1), *dma(1),
        *dma(2, 4), *dma(2, 4), *dma(4), *dma(1),
    ]
    losses, grad_query, grad_item, factor = pl.pallas_call(
        kernel,
        out_shape=(
            jax.ShapeDtypeStruct((TOK // HALF, HALF), F32),
            jax.ShapeDtypeStruct((NY, NC, NX, LINE, DOUT), BF16),
            jax.ShapeDtypeStruct((NY, NC, NX, LINE, DOUT), BF16),
            jax.ShapeDtypeStruct((1, DOUT), F32),
        ),
        in_specs=[smem] * 2 + [anyspace] * 7 + [vmem] * 2,
        out_specs=(vmem, vmem, vmem, vmem),
        scratch_shapes=scratch,
        compiler_params=pltpu.CompilerParams(
            collective_id=0, has_side_effects=True, vmem_limit_bytes=56 * 2**20
        ),
        cost_estimate=pl.CostEstimate(flops=6_500_000_000, bytes_accessed=12_000_000, transcendentals=2_100_000),
        name="step",
    )(
        quo_bucket, rem_bucket, user_features, w_query_in, w_query_out, quo_table, rem_table, w_item_in,
        w_item_out, counts.reshape(16, HALF), positive.reshape(TOK // HALF, HALF),
    )
    def scaled(grad):
        return grad.reshape(HID, DOUT).astype(F32) * factor

    return (losses.reshape(TOK), scaled(grad_query), scaled(grad_item))


def solution(mesh):
    in_specs = (
        P(("sec", "dev"), None), P(), P(), P("dev", None), P("dev", None), P(), P(),
        P("dev"), P("dev"), P(), P(("sec", "dev")),
    )
    out_specs = (P(("sec", "dev")), P(), P())
    return jax.shard_map(local, mesh=mesh, in_specs=in_specs, out_specs=out_specs, check_vma=False)
```

```python
import jax
import jax.numpy as jnp
from jax import lax
from jax.experimental import pallas as pl
from jax.experimental.pallas import tpu as pltpu
from jax.sharding import PartitionSpec as P

EPS = 1e-06
INV_TEMPER = 20.0
LOG2E = 1.4426950408889634
MESH = pl.DeviceIdType.MESH
F32 = jnp.float32
BF16 = jnp.bfloat16

NX, NC, NY, NZ = 4, 2, 4, 8
PLANE = NY * NZ
TOK, DIN, HID, DOUT = 1024, 1024, 1024, 256
QUARTER = 8
BLOCK = PLANE * QUARTER
SLOTS = NX * NC
SHARD = 128
TROWS = 8192
CHUNKS = 4
ZFIRST = 3
ORDER = (0, ZFIRST, 1, 2)


def hops(k, n):
    return min(k, n - k)


Z_FAR = sorted(range(1, NZ), key=lambda k: -hops(k, NZ))
WIDE = DIN // CHUNKS
TILE = 256
HALF = 128
LINE = 32
ROWS = NC * NX * LINE


def dot(a, b, ca, cb):
    return lax.dot_general(a, b, (((ca,), (cb,)), ((), ())), preferred_element_type=F32)


def norm_scale(raw):
    return lax.rsqrt(jnp.mean(raw * raw, axis=-1, keepdims=True) + EPS)


def norm_vjp(raw, grad):
    r = norm_scale(raw)
    dotted = jnp.mean(grad * raw, axis=-1, keepdims=True)
    return (grad * r - raw * (r * r * r * dotted)) * (DOUT**-0.5)


def stack(rows):
    n = rows.shape[0] // 8
    left = rows[:, :HALF].reshape(n, 8, HALF)
    right = rows[:, HALF:].reshape(n, 8, HALF)
    return jnp.concatenate([left, right], axis=1)


def unstack(tiles):
    n = tiles.shape[0]
    left = tiles[:, :8, :].reshape(n * 8, HALF)
    right = tiles[:, 8:, :].reshape(n * 8, HALF)
    return left, right


GRAY = (0, 1, 3, 2)


def kernel(
    quo_idx, rem_idx, feat_hbm, wqi_hbm, wqo_hbm, quo_hbm, rem_hbm, wii_hbm, wio_hbm, counts_in, pos_in,
    loss_ref, fin_query, fin_item, factor_ref,
    feat, wqi, wqo, tab, wii, wio,
    idx_out, idx_recv, sel, srow, rrow, zrow, rzrow, srz, rrz, sry, rry, pre,
    hq, qraw, qv, xall, gv, hz, hsrc, hcol,
    est, esum, psum, posb, invb, gall, tsrc, rc, sx, rx, town, sg, rg,
    rgv, arc, aown, asx, arx,
    qfull, qsrc, qrc, qsx, qrx, qsy, qry, qz,
    lc_ref,
    load_sem,
    idx_ss, idx_rs, tab_ss, tab_rs, ry_ss, ry_rs, rz_ss, rz_rs, rf_ss, rf_rs, rl_ss, rl_rs,
    vp_ss, vp_rs, vx_ss, vx_rs, vc_ss, vc_rs,
    hz_ss, hz_rs, hy_ss, hy_rs,
    tc_ss, tc_rs, tx_ss, tx_rs, tp_ss, tp_rs,
    gp_ss, gp_rs,
    ac_ss, ac_rs, ax_ss, ax_rs,
    qc_ss, qc_rs, qx_ss, qx_rs, qy_ss, qy_rs, qz_ss, qz_rs,
    f_ss, f_rs, fc_ss, fc_rs,
):
    sec = lax.axis_index("sec")
    dev = lax.axis_index("dev")
    xh, c = sec // 2, sec % 2
    z, y, xl = dev // 8, (dev // 2) % 4, dev % 2
    x = xh * 2 + xl
    slot = x * 2 + c
    mine = y * NZ + z
    oc = 1 - c

    def at(ax, ac, ay, az):
        return ((ax // 2) * 2 + ac, (az * NY + ay) * 2 + ax % 2)

    def zp(k):
        return at(x, c, y, (z + k) % NZ)

    def yp(k):
        return at(x, c, (y + k) % NY, z)

    def xp(k):
        return at((x + k) % NX, c, y, z)

    other = at(x, oc, y, z)
    plane = [(ky, kz) for ky in range(NY) for kz in range(NZ) if ky or kz]
    plane.sort(key=lambda p: -hops(p[0], NY) - hops(p[1], NZ))
    sheet = [(kx, ky) for ky in range(NY) for kx in range(NX) if kx or ky]
    sheet.sort(key=lambda p: -hops(p[0], NX) - hops(p[1], NY))

    def sp(kx, ky):
        return at((x + kx) % NX, c, (y + ky) % NY, z)

    def pp(i):
        ky, kz = plane[i]
        return at(x, c, (y + ky) % NY, (z + kz) % NZ)

    def pg(i):
        ky, kz = plane[i]
        return ((y + ky) % NY) * NZ + (z + kz) % NZ

    partner_x = jnp.where(c == 0, x + 1 - 2 * (x % 2), (x + 3 + 2 * (x % 2)) % NX)
    partner = at(partner_x, c, y, z)
    fin = (fin_query, fin_item)
    sent = []

    def copy(src, dst, ss, rs, target):
        return pltpu.make_async_remote_copy(
            src_ref=src, dst_ref=dst, send_sem=ss, recv_sem=rs, device_id=target, device_id_type=MESH
        )

    def push(src, dst, ss, rs, target):
        cp = copy(src, dst, ss, rs, target)
        cp.start()
        sent.append(cp)
        return cp

    def landed(region, rs):
        copy(region, region, rs, rs, other).wait_recv()

    def left_here(region, ss):
        sent.append(copy(region, region, ss, ss, other))

    def flush():
        for cp in sent:
            cp.wait_send()
        sent.clear()

    barrier = pltpu.get_barrier_semaphore()
    for i in range(len(plane)):
        pl.semaphore_signal(barrier, inc=1, device_id=pp(i), device_id_type=MESH)
    greeted = len(plane) + 1
    pl.semaphore_signal(barrier, inc=1, device_id=other, device_id_type=MESH)
    for kx, ky in sheet:
        if kx:
            greeted += 1
            pl.semaphore_signal(barrier, inc=1, device_id=sp(kx, ky), device_id_type=MESH)

    loads = []

    def load(src, dst):
        cp = pltpu.make_async_copy(src, dst, load_sem.at[len(loads)])
        cp.start()
        loads.append(cp)

    for ch in range(CHUNKS):
        load(quo_hbm.at[:, ch * WIDE : (ch + 1) * WIDE], tab.at[ch, pl.ds(0, SHARD)])
        load(rem_hbm.at[:, ch * WIDE : (ch + 1) * WIDE], tab.at[ch, pl.ds(2 * SHARD, SHARD)])
    for src, dst in ((feat_hbm, feat), (wqi_hbm, wqi), (wqo_hbm, wqo), (wii_hbm, wii), (wio_hbm, wio)):
        load(src, dst)

    lane = lax.broadcasted_iota(jnp.int32, (NY, HALF), 1) - z * 2 * QUARTER
    lane = jnp.where(lax.broadcasted_iota(jnp.int32, (NY, HALF), 0) == y, lane, -1)
    asked = jnp.zeros((NY, HALF), jnp.int32)
    for j in range(QUARTER):
        asked = jnp.where(lane == j, quo_idx[sec * QUARTER + j], asked)
        asked = jnp.where(lane == QUARTER + j, rem_idx[sec * QUARTER + j] + TROWS, asked)
    idx_out[...] = asked
    for i in range(2 * CHUNKS):
        loads[i].wait()
    pl.semaphore_wait(barrier, greeted)

    own_rows = pl.ds(pl.multiple_of(c * 2 * SHARD, SHARD), SHARD)
    their_rows = pl.ds(pl.multiple_of(c * 2 * SHARD + SHARD, SHARD), SHARD)

    def tab_copy(ch):
        return copy(
            tab.at[ch, own_rows], tab.at[ch, their_rows], tab_ss.at[0, ch], tab_rs.at[0, ch], partner
        )

    def tab_core_copy(ch):
        return copy(
            tab.at[ch, their_rows], tab.at[ch, their_rows], tab_ss.at[1, ch], tab_rs.at[1, ch], other
        )

    for ch in ORDER:
        tab_copy(ch).start()
    for i in range(len(plane)):
        copy(idx_out, idx_recv.at[i], idx_ss.at[0], idx_rs.at[0], pp(i)).start()
    left_here(idx_recv, idx_ss.at[0])

    pos = pos_in[...]
    place = ((pos // 16) % 2) * 1024 + ((pos // 32) % 2) * 512 + ((pos // 8) % 2) * 256
    place = place + ((pos // 64) % 4) * 64 + (pos // 256) * 8 + pos % 8
    place = place.T
    for i in range(TOK // HALF):
        posb[pl.ds(i * HALF, HALF), :] = jnp.broadcast_to(place[:, i : i + 1], (HALF, HALF))

    counts = counts_in[...]
    high = (counts // 8).astype(F32).astype(BF16)
    low = (counts % 8).astype(F32).astype(BF16)
    src = lax.broadcasted_iota(jnp.int32, (HALF, BLOCK), 0)
    dst = lax.broadcasted_iota(jnp.int32, (HALF, BLOCK), 1)
    src = jnp.where((src // 64 == (dst // 64) % 2) & (src % 8 == dst % 8), (src // 8) % 8, -1)
    down = lax.broadcasted_iota(jnp.int32, (16, BLOCK), 0)
    dst = lax.broadcasted_iota(jnp.int32, (16, BLOCK), 1)
    keep = down == ((dst // 8) % 8) * 2 + dst // HALF
    for s in range(SLOTS):
        pick = (src == (s // 2 % 2) * 4 + (s // 4) * 2 + s % 2).astype(F32).astype(BF16)
        wide = dot(high, pick, 1, 0) * 8.0 + dot(low, pick, 1, 0)
        lc_ref[s] = jnp.log(jnp.sum(jnp.where(keep, wide, 0.0), axis=0, keepdims=True)) * LOG2E

    loads[2 * CHUNKS].wait()
    loads[2 * CHUNKS + 1].wait()

    hq[...] = jnp.maximum(dot(feat[...], wqi[...], 1, 0), 0.0).astype(BF16)

    tab_copy(ORDER[0]).wait_recv()
    tab_core_copy(ORDER[0]).start()
    landed(idx_recv, idx_rs.at[0])
    total = idx_out[...]
    for i in range(len(plane)):
        total = total + idx_recv[i]
    total = jnp.concatenate([total, jnp.zeros((8 - NY, HALF), jnp.int32)], axis=0).T
    line = lax.broadcasted_iota(jnp.int32, (HALF, 4 * SHARD), 1)
    which = line // SHARD
    owner = jnp.where(which % 2 == 0, dev, dev + 1 - 2 * xl)
    row_id = line % SHARD + owner * SHARD + (which // 2) * TROWS
    for i in range(NY):
        sel[i] = (row_id == total[:, i : i + 1]).astype(F32).astype(BF16)

    def row_copy(ch, k):
        return copy(srow.at[ch, k], rrow.at[ch, k - 1], ry_ss.at[ch], ry_rs.at[ch], yp(k))

    for i, ch in enumerate(ORDER):
        if i < CHUNKS - 1:
            tab_copy(ORDER[i + 1]).wait_recv()
            tab_core_copy(ORDER[i + 1]).start()
        tab_core_copy(ch).wait_recv()
        if ch == ZFIRST:
            for i in range(NY):
                got = dot(sel[i], tab[ch], 1, 0).astype(BF16)
                srz[:, i * 16 : (i + 1) * 16, :] = got.reshape(NZ, 16, WIDE)
            for k in Z_FAR:
                copy(srz.at[(z + k) % NZ], rrz.at[k - 1], rf_ss.at[0], rf_rs.at[0], zp(k)).start()
            left_here(rrz, rf_ss.at[0])
        else:
            for k in (2, 1, 3, 0):
                srow[ch, k] = dot(sel[(y + k) % NY], tab[ch], 1, 0).astype(BF16)
                if k:
                    row_copy(ch, k).start()
            left_here(rrow.at[ch], ry_ss.at[ch])
        sent.append(tab_copy(ch))
        sent.append(tab_core_copy(ch))

    loads[2 * CHUNKS + 2].wait()

    raw = dot(hq[...], wqo[...], 1, 0)
    qraw[...] = raw
    qv[...] = (raw * norm_scale(raw) * (DOUT**-0.5)).astype(BF16)

    def zrow_copy(ch, k):
        return copy(
            zrow.at[ch, (z + k) % NZ], rzrow.at[ch, k - 1], rz_ss.at[ch], rz_rs.at[ch], zp(k)
        )

    def along_z(ch):
        landed(rrow.at[ch], ry_rs.at[ch])
        s = srow[ch, 0].astype(F32)
        for k in range(NY - 1):
            s = s + rrow[ch, k].astype(F32)
        zrow[ch] = s.astype(BF16).reshape(NZ, 16, WIDE)
        for k in Z_FAR:
            zrow_copy(ch, k).start()
        left_here(rzrow.at[ch], rz_ss.at[ch])

    along_z(0)
    along_z(1)
    landed(rrz, rf_rs.at[0])
    s = srz[z].astype(F32)
    for k in range(NZ - 1):
        s = s + rrz[k].astype(F32)
    sry[...] = s.astype(BF16).reshape(NY, 16, WIDE)
    for k in (2, 1, 3):
        copy(sry.at[(y + k) % NY], rry.at[k - 1], rl_ss.at[0], rl_rs.at[0], yp(k)).start()
    left_here(rry, rl_ss.at[0])
    along_z(2)

    loads[2 * CHUNKS + 3].wait()
    loads[2 * CHUNKS + 4].wait()
    pre[...] = jnp.zeros_like(pre)

    for ch in (0, 1, ZFIRST, 2):
        if ch == ZFIRST:
            landed(rry, rl_rs.at[0])
            s = sry[y].astype(F32)
            for k in range(NY - 1):
                s = s + rry[k].astype(F32)
        else:
            landed(rzrow.at[ch], rz_rs.at[ch])
            s = zrow[ch, z].astype(F32)
            for k in range(NZ - 1):
                s = s + rzrow[ch, k].astype(F32)
        emb = s[:8] * s[8:]
        emb = jnp.concatenate([emb, emb], axis=0).astype(BF16)
        pre[...] += dot(emb, wii[ch * WIDE : (ch + 1) * WIDE, :], 1, 0)

    hid = jnp.maximum(pre[...], 0.0).astype(BF16)
    iraw = dot(hid, wio[...], 1, 0)[:8]
    ivec = iraw * norm_scale(iraw) * (DOUT**-0.5)
    gv[mine] = stack(ivec)[0].astype(BF16)

    for i in range(len(plane)):
        copy(gv.at[mine], gv.at[mine], vp_ss.at[0], vp_rs.at[0], pp(i)).start()
    flush()
    left_here(gv.at[pl.ds(0, PLANE - 1)], vp_ss.at[0])
    hid8 = hid.astype(F32)[:8]
    hz[z] = jnp.concatenate([hid8[:, :512], hid8[:, 512:]], axis=0).astype(BF16)
    esum[...] = jnp.zeros_like(esum)
    psum[...] = jnp.zeros_like(psum)
    landed(gv.at[pl.ds(0, PLANE - 1)], vp_rs.at[0])
    left, right = unstack(gv[...].astype(F32))
    xall[slot, :, :HALF] = left.astype(BF16)
    xall[slot, :, HALF:] = right.astype(BF16)

    def vx_copy(k):
        return copy(xall.at[slot], xall.at[slot], vx_ss.at[k - 1], vx_rs.at[k - 1], xp(k))

    for k in (1, 3, 2):
        vx_copy(k).start()
    for k in Z_FAR:
        copy(hz.at[z], hz.at[z], hz_ss.at[0], hz_rs.at[0], zp(k)).start()
    left_here(hz.at[pl.ds(0, NZ - 1)], hz_ss.at[0])

    def first_pass(s):
        logit = dot(qv[...], xall[s], 1, 1) * (INV_TEMPER * LOG2E) - lc_ref[s]
        e = jnp.exp2(logit)
        est[s] = e
        esum[...] += e[:, :HALF] + e[:, HALF:]
        lanes = lax.broadcasted_iota(jnp.int32, (TOK, HALF), 1)
        target = posb[...] - s * BLOCK
        hit = jnp.where(target == lanes, logit[:, :HALF], 0.0)
        hit = jnp.where(target == lanes + HALF, logit[:, HALF:], hit)
        psum[...] += hit

    def vc_copy(p):
        s = ((x + NX - GRAY[p]) % NX) * 2 + c
        return copy(xall.at[s], xall.at[s], vc_ss.at[p], vc_rs.at[p], other)

    for p in range(NX):
        if p:
            vx_copy(GRAY[p]).wait_recv()
        s = ((x + NX - GRAY[p]) % NX) * 2
        vc_copy(p).start()
        first_pass(s + c)
        vc_copy(p).wait_recv()
        first_pass(s + oc)

    landed(hz.at[pl.ds(0, NZ - 1)], hz_rs.at[0])
    hv = hz[...].astype(F32)
    hv = jnp.concatenate([hv[:, :8, :].reshape(64, 512), hv[:, 8:, :].reshape(64, 512)], axis=1)
    hv = hv.astype(BF16)
    for i in range(NY):
        hsrc[i] = hv[:, i * ROWS : (i + 1) * ROWS]
    hcol[y] = hsrc[y]
    for k in range(1, NY):
        copy(hsrc.at[(y + k) % NY], hcol.at[y], hy_ss.at[0], hy_rs.at[0], yp(k)).start()
    left_here(hcol.at[pl.ds(0, NY - 1)], hy_ss.at[0])
    sums = jnp.sum(esum[...], axis=1, keepdims=True)
    picked = jnp.sum(psum[...], axis=1, keepdims=True)
    invb[...] = jnp.broadcast_to(1.0 / sums, (TOK, HALF))
    loss = (jnp.log2(sums) - picked) * (1.0 / LOG2E)
    loss = jnp.broadcast_to(loss, (TOK, HALF)).reshape(TOK // HALF, HALF, HALF)
    down = lax.broadcasted_iota(jnp.int32, (TOK // HALF, HALF, HALF), 1)
    across = lax.broadcasted_iota(jnp.int32, (TOK // HALF, HALF, HALF), 2)
    loss_ref[...] = jnp.sum(jnp.where(down == across, loss, 0.0), axis=1)

    def weigh(s):
        lanes = lax.broadcasted_iota(jnp.int32, (TOK, HALF), 1)
        target = posb[...] - s * BLOCK
        scale = invb[...]
        pa = est[s, :, :HALF] * scale
        pb = est[s, :, HALF:] * scale
        gall[s, :, :HALF] = jnp.where(target == lanes, pa - 1.0, pa).astype(BF16)
        gall[s, :, HALF:] = jnp.where(target == lanes + HALF, pb - 1.0, pb).astype(BF16)

    def spread(s):
        return dot(gall[s], qv[...], 0, 0) * INV_TEMPER

    def tc_copy(k):
        return copy(tsrc.at[k], rc.at[k], tc_ss.at[k], tc_rs.at[k], other)

    def tx_copy(k):
        return copy(sx.at[k], rx.at[k - 1], tx_ss.at[0], tx_rs.at[0], xp(k))

    def settle(k):
        tc_copy(k).wait_recv()
        t = town[k] + rc[k].astype(F32)
        if k:
            sx[k] = t.astype(BF16)
            tx_copy(k).start()
        else:
            town[k] = t

    turns = (2, 1, 3, 0)
    for p, k in enumerate(turns):
        s = ((x + k) % NX) * 2
        weigh(s + oc)
        weigh(s + c)
        tsrc[k] = spread(s + oc).astype(BF16)
        tc_copy(k).start()
        if p:
            settle(turns[p - 1])
        town[k] = spread(s + c)
    settle(0)

    acc = dot(gall[0], xall[0], 1, 0)
    for s in range(1, SLOTS):
        acc = acc + dot(gall[s], xall[s], 1, 0)
    qv[...] = norm_vjp(qraw[...], acc * INV_TEMPER).astype(BF16)

    qfull[...] = dot(hq[...], qv[...], 0, 0)

    def core_rows(i, core):
        return pl.ds(pl.multiple_of(i * ROWS + core * HALF, HALF), HALF)

    for i in range(NY):
        qsrc[i] = qfull[core_rows(i, oc), :].astype(BF16)
    qc_cp = push(qsrc, qrc, qc_ss.at[0], qc_rs.at[0], other)

    flush()
    for k in range(1, NX):
        sent.append(vx_copy(k))
    for k in range(NX):
        sent.append(vc_copy(k))
        sent.append(tc_copy(k))
    left_here(rx, tx_ss.at[0])
    landed(rx, tx_rs.at[0])
    t = town[0]
    for k in range(NX - 1):
        t = t + rx[k].astype(F32)
    sg[...] = stack(t).astype(BF16)
    for i in range(len(plane)):
        copy(sg.at[pg(i)], rg.at[i], tp_ss.at[0], tp_rs.at[0], pp(i)).start()

    qc_cp.wait_recv()
    for i in range(NY):
        q = qfull[core_rows(i, c), :] + qrc[i].astype(F32)
        qsx[:, i] = q.reshape(NX, LINE, DOUT).astype(BF16)
    for k in (1, 3, 2):
        copy(qsx.at[(x + k) % NX], qrx.at[k - 1], qx_ss.at[0], qx_rs.at[0], xp(k)).start()
    flush()
    left_here(rg, tp_ss.at[0])
    left_here(qrx, qx_ss.at[0])

    landed(rg, tp_rs.at[0])
    t = sg[mine].astype(F32)
    for i in range(len(plane)):
        t = t + rg[i].astype(F32)
    t = jnp.concatenate([t[:8], t[8:]], axis=1)
    rgv[mine] = stack(norm_vjp(iraw, t))[0].astype(BF16)
    for i in range(len(plane)):
        copy(rgv.at[mine], rgv.at[mine], gp_ss.at[0], gp_rs.at[0], pp(i)).start()

    landed(qrx, qx_rs.at[0])
    q = qsx[x].astype(F32)
    for k in range(NX - 1):
        q = q + qrx[k].astype(F32)
    qsy[...] = q.astype(BF16)
    for k in range(1, NY):
        copy(qsy.at[(y + k) % NY], qry.at[k - 1], qy_ss.at[0], qy_rs.at[0], yp(k)).start()
    flush()
    left_here(rgv.at[pl.ds(0, PLANE - 1)], gp_ss.at[0])
    left_here(qry, qy_ss.at[0])

    landed(qry, qy_rs.at[0])
    q = qsy[y].astype(F32)
    for k in range(NY - 1):
        q = q + qry[k].astype(F32)
    qz[z] = q.astype(BF16)
    for k in Z_FAR:
        copy(qz.at[z], qz.at[z], qz_ss.at[0], qz_rs.at[0], zp(k)).start()
    left_here(qz.at[pl.ds(0, NZ - 1)], qz_ss.at[0])

    landed(hcol.at[pl.ds(0, NY - 1)], hy_rs.at[0])
    landed(rgv.at[pl.ds(0, PLANE - 1)], gp_rs.at[0])
    left, right = unstack(rgv[...].astype(F32))
    raw_grad = jnp.concatenate([left, right], axis=1).astype(BF16)
    aown[...] = dot(hcol[...].reshape(BLOCK, ROWS), raw_grad, 0, 0)
    ac_cp = push(aown.at[core_rows(0, oc)], arc, ac_ss.at[0], ac_rs.at[0], other)

    ac_cp.wait_recv()
    asx[...] = (aown[core_rows(0, c), :] + arc[...]).reshape(NX, LINE, DOUT)
    for k in (2, 1, 3):
        copy(asx.at[(x + k) % NX], arx.at[k - 1], ax_ss.at[0], ax_rs.at[0], xp(k)).start()
    flush()
    left_here(arx, ax_ss.at[0])

    def square_sum(m):
        v = fin[m][...].reshape(HID, DOUT).astype(F32)
        v = jnp.sum((v * v).reshape(HID // 8, 8, DOUT), axis=0)
        return v[:, :HALF] + v[:, HALF:]

    def group(ref, ky, lead):
        return ref.at[lead + (pl.ds(0, NX - 1),)] if ky == 0 else ref.at[lead]

    def gather(m):
        for kx, ky in sheet:
            copy(
                fin[m].at[y, c, x], fin[m].at[y, c, x], f_ss.at[m, ky], f_rs.at[m, ky], sp(kx, ky)
            ).start()
        for ky in range(NY):
            left_here(group(fin[m], ky, (0, 0)), f_ss.at[m, ky])

    def gather_core(m):
        for ky in range(NY):
            landed(group(fin[m], ky, (0, 0)), f_rs.at[m, ky])
            block = fin[m].at[(y + NY - ky) % NY, c]
            fc_cp.append(push(block, block, fc_ss.at[m, ky], fc_rs.at[m, ky], other))

    fc_cp = []

    landed(qz.at[pl.ds(0, NZ - 1)], qz_rs.at[0])
    q = qz[0].astype(F32)
    for k in range(1, NZ):
        q = q + qz[k].astype(F32)
    fin_query[y, c, x] = q.astype(BF16)
    gather(0)

    landed(arx, ax_rs.at[0])
    a = asx[x]
    for k in range(NX - 1):
        a = a + arx[k]
    fin_item[y, c, x] = a.astype(BF16)
    gather(1)
    gather_core(0)
    flush()
    for cp in fc_cp:
        cp.wait_recv()
    square = square_sum(0)
    gather_core(1)
    for cp in fc_cp[NY:]:
        cp.wait_recv()
    square = square + square_sum(1)
    square = jnp.sum(square, axis=0, keepdims=True)
    norm = jnp.sqrt(jnp.sum(square, axis=1, keepdims=True))
    limit = (HID * DOUT / 2) ** 0.5
    factor_ref[...] = jnp.broadcast_to(limit / jnp.maximum(norm, limit), (1, DOUT))
    flush()


def finish(loss_in, query_in, item_in, factor_in, loss_out, query_out, item_out):
    loss_out[...] = loss_in[...]
    query_out[...] = query_in[...].reshape(HID, DOUT).astype(F32) * factor_in[...]
    item_out[...] = item_in[...].reshape(HID, DOUT).astype(F32) * factor_in[...]


def local(
    user_features, w_query_in, w_query_out, quo_table, rem_table, w_item_in, w_item_out,
    quo_bucket, rem_bucket, counts, positive,
):
    def vm(*shape, dtype=BF16):
        return pltpu.VMEM(shape, dtype)

    def dma(*shape):
        return [pltpu.SemaphoreType.DMA(shape)] * 2

    anyspace = pl.BlockSpec(memory_space=pl.ANY)
    vmem = pl.BlockSpec(memory_space=pltpu.VMEM)
    smem = pl.BlockSpec(memory_space=pltpu.SMEM)
    scratch = [
        vm(TOK, DIN), vm(DIN, HID), vm(HID, DOUT), vm(CHUNKS, 4 * SHARD, WIDE), vm(DIN, HID), vm(HID, DOUT),
        vm(NY, HALF, dtype=jnp.int32), vm(PLANE - 1, NY, HALF, dtype=jnp.int32), vm(NY, HALF, 4 * SHARD),
        vm(CHUNKS - 1, NY, HALF, WIDE), vm(CHUNKS - 1, NY - 1, HALF, WIDE),
        vm(CHUNKS - 1, NZ, 16, WIDE), vm(CHUNKS - 1, NZ - 1, 16, WIDE),
        vm(NZ, NY * 16, WIDE), vm(NZ - 1, NY * 16, WIDE), vm(NY, 16, WIDE), vm(NY - 1, 16, WIDE),
        vm(16, HID, dtype=F32),
        vm(TOK, HID), vm(TOK, DOUT, dtype=F32), vm(TOK, DOUT),
        vm(SLOTS, BLOCK, DOUT), vm(PLANE, 16, HALF), vm(NZ, 16, 512), vm(NY, 64, ROWS), vm(NY, 64, ROWS),
        vm(SLOTS, TOK, BLOCK, dtype=F32), vm(TOK, HALF, dtype=F32), vm(TOK, HALF, dtype=F32),
        vm(TOK, HALF, dtype=jnp.int32), vm(TOK, HALF, dtype=F32), vm(SLOTS, TOK, BLOCK),
        vm(NX, BLOCK, DOUT), vm(NX, BLOCK, DOUT), vm(NX, BLOCK, DOUT), vm(NX - 1, BLOCK, DOUT),
        vm(NX, BLOCK, DOUT, dtype=F32), vm(PLANE, 16, HALF), vm(PLANE - 1, 16, HALF),
        vm(PLANE, 16, HALF), vm(HALF, DOUT, dtype=F32), vm(ROWS, DOUT, dtype=F32),
        vm(NX, LINE, DOUT, dtype=F32), vm(NX - 1, LINE, DOUT, dtype=F32),
        vm(HID, DOUT, dtype=F32), vm(NY, HALF, DOUT), vm(NY, HALF, DOUT),
        vm(NX, NY, LINE, DOUT), vm(NX - 1, NY, LINE, DOUT), vm(NY, LINE, DOUT), vm(NY - 1, LINE, DOUT),
        vm(NZ, LINE, DOUT),
        vm(SLOTS, 1, BLOCK, dtype=F32),
        pltpu.SemaphoreType.DMA((2 * CHUNKS + 5,)),
        *dma(1), *dma(2, CHUNKS), *dma(CHUNKS - 1), *dma(CHUNKS - 1), *dma(1), *dma(1),
        *dma(1), *dma(3), *dma(4),
        *dma(1), *dma(1),
        *dma(4), *dma(1), *dma(1),
        *dma(1),
        *dma(1), *dma(1),
        *dma(1), *dma(1), *dma(1), *dma(1),
        *dma(2, 4), *dma(2, 4),
    ]
    losses, grad_query, grad_item, factor = pl.pallas_call(
        kernel,
        out_shape=(
            jax.ShapeDtypeStruct((TOK // HALF, HALF), F32),
            jax.ShapeDtypeStruct((NY, NC, NX, LINE, DOUT), BF16),
            jax.ShapeDtypeStruct((NY, NC, NX, LINE, DOUT), BF16),
            jax.ShapeDtypeStruct((1, DOUT), F32),
        ),
        in_specs=[smem] * 2 + [anyspace] * 7 + [vmem] * 2,
        out_specs=(vmem, vmem, vmem, vmem),
        scratch_shapes=scratch,
        compiler_params=pltpu.CompilerParams(
            collective_id=0, has_side_effects=True, vmem_limit_bytes=56 * 2**20
        ),
        cost_estimate=pl.CostEstimate(flops=6_500_000_000, bytes_accessed=12_000_000, transcendentals=2_100_000),
        name="step",
    )(
        quo_bucket, rem_bucket, user_features, w_query_in, w_query_out, quo_table, rem_table, w_item_in,
        w_item_out, counts.reshape(16, HALF), positive.reshape(TOK // HALF, HALF),
    )
    losses, grad_query, grad_item = pl.pallas_call(
        finish,
        out_shape=(
            jax.ShapeDtypeStruct((TOK // HALF, HALF), F32),
            jax.ShapeDtypeStruct((HID, DOUT), F32),
            jax.ShapeDtypeStruct((HID, DOUT), F32),
        ),
        in_specs=[vmem] * 4,
        out_specs=(vmem, vmem, vmem),
        name="scale",
    )(losses, grad_query, grad_item, factor)
    return (losses.reshape(TOK), grad_query, grad_item)


def solution(mesh):
    in_specs = (
        P(("sec", "dev"), None), P(), P(), P("dev", None), P("dev", None), P(), P(),
        P("dev"), P("dev"), P(), P(("sec", "dev")),
    )
    out_specs = (P(("sec", "dev")), P(), P())
    return jax.shard_map(local, mesh=mesh, in_specs=in_specs, out_specs=out_specs, check_vma=False)
```

```python
import jax
import jax.numpy as jnp
from jax import lax
from jax.experimental import pallas as pl
from jax.experimental.pallas import tpu as pltpu
from jax.sharding import PartitionSpec as P

EPS = 1e-06
INV_TEMPER = 20.0
LOG2E = 1.4426950408889634
MESH = pl.DeviceIdType.MESH
F32 = jnp.float32
BF16 = jnp.bfloat16

NX, NC, NY, NZ = 4, 2, 4, 8
PLANE = NY * NZ
TOK, DIN, HID, DOUT = 1024, 1024, 1024, 256
QUARTER = 8
BLOCK = PLANE * QUARTER
SLOTS = NX * NC
SHARD = 128
TROWS = 8192
CHUNKS = 4
ZFIRST = 3
ORDER = (0, ZFIRST, 1, 2)


def hops(k, n):
    return min(k, n - k)


Z_FAR = sorted(range(1, NZ), key=lambda k: -hops(k, NZ))
WIDE = DIN // CHUNKS
TILE = 256
HALF = 128
LINE = 32
ROWS = NC * NX * LINE


def dot(a, b, ca, cb):
    return lax.dot_general(a, b, (((ca,), (cb,)), ((), ())), preferred_element_type=F32)


def norm_scale(raw):
    return lax.rsqrt(jnp.mean(raw * raw, axis=-1, keepdims=True) + EPS)


def norm_vjp(raw, grad):
    r = norm_scale(raw)
    dotted = jnp.mean(grad * raw, axis=-1, keepdims=True)
    return (grad * r - raw * (r * r * r * dotted)) * (DOUT**-0.5)


def stack(rows):
    n = rows.shape[0] // 8
    left = rows[:, :HALF].reshape(n, 8, HALF)
    right = rows[:, HALF:].reshape(n, 8, HALF)
    return jnp.concatenate([left, right], axis=1)


def unstack(tiles):
    n = tiles.shape[0]
    left = tiles[:, :8, :].reshape(n * 8, HALF)
    right = tiles[:, 8:, :].reshape(n * 8, HALF)
    return left, right


GRAY = (0, 1, 3, 2)


def kernel(
    quo_idx_hbm, rem_idx_hbm, feat_hbm, wqi_hbm, wqo_hbm, quo_hbm, rem_hbm, wii_hbm, wio_hbm, counts_hbm,
    pos_hbm,
    loss_ref, fin_query, fin_item, factor_ref,
    quo_idx, rem_idx, counts_in, pos_in, feat, wqi, wqo, tab, wii, wio,
    idx_out, idx_recv, sel, srow, rrow, zrow, rzrow, srz, rrz, sry, rry, pre,
    hq, qraw, qv, xall, gv, hz, hsrc, hcol,
    est, esum, psum, posb, invb, gall, tsrc, rc, sx, rx, town, sg, rg,
    rgv, arc, aown, asx, arx,
    qfull, qsrc, qrc, qsx, qrx, qsy, qry, qz,
    lc_ref,
    load_sem,
    idx_ss, idx_rs, tab_ss, tab_rs, ry_ss, ry_rs, rz_ss, rz_rs, rf_ss, rf_rs, rl_ss, rl_rs,
    vp_ss, vp_rs, vx_ss, vx_rs, vc_ss, vc_rs,
    hz_ss, hz_rs, hy_ss, hy_rs,
    tc_ss, tc_rs, tx_ss, tx_rs, tp_ss, tp_rs,
    gp_ss, gp_rs,
    ac_ss, ac_rs, ax_ss, ax_rs,
    qc_ss, qc_rs, qx_ss, qx_rs, qy_ss, qy_rs, qz_ss, qz_rs,
    f_ss, f_rs, fc_ss, fc_rs,
):
    sec = lax.axis_index("sec")
    dev = lax.axis_index("dev")
    xh, c = sec // 2, sec % 2
    z, y, xl = dev // 8, (dev // 2) % 4, dev % 2
    x = xh * 2 + xl
    slot = x * 2 + c
    mine = y * NZ + z
    oc = 1 - c

    def at(ax, ac, ay, az):
        return ((ax // 2) * 2 + ac, (az * NY + ay) * 2 + ax % 2)

    def zp(k):
        return at(x, c, y, (z + k) % NZ)

    def yp(k):
        return at(x, c, (y + k) % NY, z)

    def xp(k):
        return at((x + k) % NX, c, y, z)

    other = at(x, oc, y, z)
    plane = [(ky, kz) for ky in range(NY) for kz in range(NZ) if ky or kz]
    plane.sort(key=lambda p: -hops(p[0], NY) - hops(p[1], NZ))
    sheet = [(kx, ky) for ky in range(NY) for kx in range(NX) if kx or ky]
    sheet.sort(key=lambda p: -hops(p[0], NX) - hops(p[1], NY))

    def sp(kx, ky):
        return at((x + kx) % NX, c, (y + ky) % NY, z)

    def pp(i):
        ky, kz = plane[i]
        return at(x, c, (y + ky) % NY, (z + kz) % NZ)

    def pg(i):
        ky, kz = plane[i]
        return ((y + ky) % NY) * NZ + (z + kz) % NZ

    partner_x = jnp.where(c == 0, x + 1 - 2 * (x % 2), (x + 3 + 2 * (x % 2)) % NX)
    partner = at(partner_x, c, y, z)
    fin = (fin_query, fin_item)
    sent = []

    def copy(src, dst, ss, rs, target):
        return pltpu.make_async_remote_copy(
            src_ref=src, dst_ref=dst, send_sem=ss, recv_sem=rs, device_id=target, device_id_type=MESH
        )

    def push(src, dst, ss, rs, target):
        cp = copy(src, dst, ss, rs, target)
        cp.start()
        sent.append(cp)
        return cp

    def landed(region, rs):
        copy(region, region, rs, rs, other).wait_recv()

    def left_here(region, ss):
        sent.append(copy(region, region, ss, ss, other))

    def flush():
        for cp in sent:
            cp.wait_send()
        sent.clear()

    barrier = pltpu.get_barrier_semaphore()
    for i in range(len(plane)):
        pl.semaphore_signal(barrier, inc=1, device_id=pp(i), device_id_type=MESH)
    greeted = len(plane) + 1
    pl.semaphore_signal(barrier, inc=1, device_id=other, device_id_type=MESH)
    for kx, ky in sheet:
        if kx:
            greeted += 1
            pl.semaphore_signal(barrier, inc=1, device_id=sp(kx, ky), device_id_type=MESH)

    loads = []

    def load(src, dst):
        cp = pltpu.make_async_copy(src, dst, load_sem.at[len(loads)])
        cp.start()
        loads.append(cp)
        return cp

    first = [load(quo_idx_hbm, quo_idx), load(rem_idx_hbm, rem_idx)]
    shards = []
    for ch in range(CHUNKS):
        shards.append(load(quo_hbm.at[:, ch * WIDE : (ch + 1) * WIDE], tab.at[ch, pl.ds(0, SHARD)]))
        shards.append(load(rem_hbm.at[:, ch * WIDE : (ch + 1) * WIDE], tab.at[ch, pl.ds(2 * SHARD, SHARD)]))
    small = [load(pos_hbm, pos_in), load(counts_hbm, counts_in)]
    matrices = ((feat_hbm, feat), (wqi_hbm, wqi), (wqo_hbm, wqo), (wii_hbm, wii), (wio_hbm, wio))
    large = [load(src, dst) for src, dst in matrices]

    lane = lax.broadcasted_iota(jnp.int32, (NY, HALF), 1) - z * 2 * QUARTER
    lane = jnp.where(lax.broadcasted_iota(jnp.int32, (NY, HALF), 0) == y, lane, -1)
    for cp in first:
        cp.wait()
    asked = jnp.zeros((NY, HALF), jnp.int32)
    for j in range(QUARTER):
        asked = jnp.where(lane == j, quo_idx[sec * QUARTER + j], asked)
        asked = jnp.where(lane == QUARTER + j, rem_idx[sec * QUARTER + j] + TROWS, asked)
    idx_out[...] = asked
    for cp in shards:
        cp.wait()
    pl.semaphore_wait(barrier, greeted)

    own_rows = pl.ds(pl.multiple_of(c * 2 * SHARD, SHARD), SHARD)
    their_rows = pl.ds(pl.multiple_of(c * 2 * SHARD + SHARD, SHARD), SHARD)

    def tab_copy(ch):
        return copy(
            tab.at[ch, own_rows], tab.at[ch, their_rows], tab_ss.at[0, ch], tab_rs.at[0, ch], partner
        )

    def tab_core_copy(ch):
        return copy(
            tab.at[ch, their_rows], tab.at[ch, their_rows], tab_ss.at[1, ch], tab_rs.at[1, ch], other
        )

    for ch in ORDER:
        tab_copy(ch).start()
    for i in range(len(plane)):
        copy(idx_out, idx_recv.at[i], idx_ss.at[0], idx_rs.at[0], pp(i)).start()
    left_here(idx_recv, idx_ss.at[0])

    for cp in small:
        cp.wait()
    pos = pos_in[...]
    place = ((pos // 16) % 2) * 1024 + ((pos // 32) % 2) * 512 + ((pos // 8) % 2) * 256
    place = place + ((pos // 64) % 4) * 64 + (pos // 256) * 8 + pos % 8
    place = place.T
    for i in range(TOK // HALF):
        posb[pl.ds(i * HALF, HALF), :] = jnp.broadcast_to(place[:, i : i + 1], (HALF, HALF))

    counts = counts_in[...]
    high = (counts // 8).astype(F32).astype(BF16)
    low = (counts % 8).astype(F32).astype(BF16)
    src = lax.broadcasted_iota(jnp.int32, (HALF, BLOCK), 0)
    dst = lax.broadcasted_iota(jnp.int32, (HALF, BLOCK), 1)
    src = jnp.where((src // 64 == (dst // 64) % 2) & (src % 8 == dst % 8), (src // 8) % 8, -1)
    down = lax.broadcasted_iota(jnp.int32, (16, BLOCK), 0)
    dst = lax.broadcasted_iota(jnp.int32, (16, BLOCK), 1)
    keep = down == ((dst // 8) % 8) * 2 + dst // HALF
    for s in range(SLOTS):
        pick = (src == (s // 2 % 2) * 4 + (s // 4) * 2 + s % 2).astype(F32).astype(BF16)
        wide = dot(high, pick, 1, 0) * 8.0 + dot(low, pick, 1, 0)
        lc_ref[s] = jnp.log(jnp.sum(jnp.where(keep, wide, 0.0), axis=0, keepdims=True)) * LOG2E

    large[0].wait()
    large[1].wait()

    hq[...] = jnp.maximum(dot(feat[...], wqi[...], 1, 0), 0.0).astype(BF16)

    tab_copy(ORDER[0]).wait_recv()
    tab_core_copy(ORDER[0]).start()
    landed(idx_recv, idx_rs.at[0])
    total = idx_out[...]
    for i in range(len(plane)):
        total = total + idx_recv[i]
    total = jnp.concatenate([total, jnp.zeros((8 - NY, HALF), jnp.int32)], axis=0).T
    line = lax.broadcasted_iota(jnp.int32, (HALF, 4 * SHARD), 1)
    which = line // SHARD
    owner = jnp.where(which % 2 == 0, dev, dev + 1 - 2 * xl)
    row_id = line % SHARD + owner * SHARD + (which // 2) * TROWS
    for i in range(NY):
        sel[i] = (row_id == total[:, i : i + 1]).astype(F32).astype(BF16)

    def row_copy(ch, k):
        return copy(srow.at[ch, k], rrow.at[ch, k - 1], ry_ss.at[ch], ry_rs.at[ch], yp(k))

    for i, ch in enumerate(ORDER):
        if i < CHUNKS - 1:
            tab_copy(ORDER[i + 1]).wait_recv()
            tab_core_copy(ORDER[i + 1]).start()
        tab_core_copy(ch).wait_recv()
        if ch == ZFIRST:
            for i in range(NY):
                got = dot(sel[i], tab[ch], 1, 0).astype(BF16)
                srz[:, i * 16 : (i + 1) * 16, :] = got.reshape(NZ, 16, WIDE)
            for k in Z_FAR:
                copy(srz.at[(z + k) % NZ], rrz.at[k - 1], rf_ss.at[0], rf_rs.at[0], zp(k)).start()
            left_here(rrz, rf_ss.at[0])
        else:
            for k in (2, 1, 3, 0):
                srow[ch, k] = dot(sel[(y + k) % NY], tab[ch], 1, 0).astype(BF16)
                if k and ch != 2:
                    row_copy(ch, k).start()
            left_here(rrow.at[ch], ry_ss.at[ch])
        sent.append(tab_copy(ch))
        sent.append(tab_core_copy(ch))

    large[2].wait()

    raw = dot(hq[...], wqo[...], 1, 0)
    qraw[...] = raw
    qv[...] = (raw * norm_scale(raw) * (DOUT**-0.5)).astype(BF16)

    def zrow_copy(ch, k):
        return copy(
            zrow.at[ch, (z + k) % NZ], rzrow.at[ch, k - 1], rz_ss.at[ch], rz_rs.at[ch], zp(k)
        )

    def along_z(ch):
        landed(rrow.at[ch], ry_rs.at[ch])
        if ch == 0:
            for k in (2, 1, 3):
                row_copy(2, k).start()
        s = srow[ch, 0].astype(F32)
        for k in range(NY - 1):
            s = s + rrow[ch, k].astype(F32)
        zrow[ch] = s.astype(BF16).reshape(NZ, 16, WIDE)
        for k in Z_FAR:
            zrow_copy(ch, k).start()
        left_here(rzrow.at[ch], rz_ss.at[ch])

    along_z(0)
    along_z(1)
    landed(rrz, rf_rs.at[0])
    s = srz[z].astype(F32)
    for k in range(NZ - 1):
        s = s + rrz[k].astype(F32)
    sry[...] = s.astype(BF16).reshape(NY, 16, WIDE)
    for k in (2, 1, 3):
        copy(sry.at[(y + k) % NY], rry.at[k - 1], rl_ss.at[0], rl_rs.at[0], yp(k)).start()
    left_here(rry, rl_ss.at[0])
    along_z(2)

    large[3].wait()
    large[4].wait()
    pre[...] = jnp.zeros_like(pre)

    for ch in (0, 1, ZFIRST, 2):
        if ch == ZFIRST:
            landed(rry, rl_rs.at[0])
            s = sry[y].astype(F32)
            for k in range(NY - 1):
                s = s + rry[k].astype(F32)
        else:
            landed(rzrow.at[ch], rz_rs.at[ch])
            s = zrow[ch, z].astype(F32)
            for k in range(NZ - 1):
                s = s + rzrow[ch, k].astype(F32)
        emb = s[:8] * s[8:]
        emb = jnp.concatenate([emb, emb], axis=0).astype(BF16)
        pre[...] += dot(emb, wii[ch * WIDE : (ch + 1) * WIDE, :], 1, 0)

    hid = jnp.maximum(pre[...], 0.0).astype(BF16)
    iraw = dot(hid, wio[...], 1, 0)[:8]
    ivec = iraw * norm_scale(iraw) * (DOUT**-0.5)
    gv[mine] = stack(ivec)[0].astype(BF16)

    for i in range(len(plane)):
        copy(gv.at[mine], gv.at[mine], vp_ss.at[0], vp_rs.at[0], pp(i)).start()
    flush()
    left_here(gv.at[pl.ds(0, PLANE - 1)], vp_ss.at[0])
    hid8 = hid.astype(F32)[:8]
    hz[z] = jnp.concatenate([hid8[:, :512], hid8[:, 512:]], axis=0).astype(BF16)
    esum[...] = jnp.zeros_like(esum)
    psum[...] = jnp.zeros_like(psum)
    landed(gv.at[pl.ds(0, PLANE - 1)], vp_rs.at[0])
    left, right = unstack(gv[...].astype(F32))
    xall[slot, :, :HALF] = left.astype(BF16)
    xall[slot, :, HALF:] = right.astype(BF16)

    def vx_copy(k):
        return copy(xall.at[slot], xall.at[slot], vx_ss.at[k - 1], vx_rs.at[k - 1], xp(k))

    for k in (1, 3, 2):
        vx_copy(k).start()
    for k in Z_FAR:
        copy(hz.at[z], hz.at[z], hz_ss.at[0], hz_rs.at[0], zp(k)).start()
    left_here(hz.at[pl.ds(0, NZ - 1)], hz_ss.at[0])

    def first_pass(s):
        logit = dot(qv[...], xall[s], 1, 1) * (INV_TEMPER * LOG2E) - lc_ref[s]
        e = jnp.exp2(logit)
        est[s] = e
        esum[...] += e[:, :HALF] + e[:, HALF:]
        lanes = lax.broadcasted_iota(jnp.int32, (TOK, HALF), 1)
        target = posb[...] - s * BLOCK
        hit = jnp.where(target == lanes, logit[:, :HALF], 0.0)
        hit = jnp.where(target == lanes + HALF, logit[:, HALF:], hit)
        psum[...] += hit

    def vc_copy(p):
        s = ((x + NX - GRAY[p]) % NX) * 2 + c
        return copy(xall.at[s], xall.at[s], vc_ss.at[p], vc_rs.at[p], other)

    for p in range(NX):
        if p:
            vx_copy(GRAY[p]).wait_recv()
        s = ((x + NX - GRAY[p]) % NX) * 2
        vc_copy(p).start()
        first_pass(s + c)
        vc_copy(p).wait_recv()
        first_pass(s + oc)

    sums = jnp.sum(esum[...], axis=1, keepdims=True)
    invb[...] = jnp.broadcast_to(1.0 / sums, (TOK, HALF))

    def weigh(s):
        lanes = lax.broadcasted_iota(jnp.int32, (TOK, HALF), 1)
        target = posb[...] - s * BLOCK
        scale = invb[...]
        pa = est[s, :, :HALF] * scale
        pb = est[s, :, HALF:] * scale
        gall[s, :, :HALF] = jnp.where(target == lanes, pa - 1.0, pa).astype(BF16)
        gall[s, :, HALF:] = jnp.where(target == lanes + HALF, pb - 1.0, pb).astype(BF16)

    def spread(s):
        return dot(gall[s], qv[...], 0, 0) * INV_TEMPER

    def tc_copy(k):
        return copy(tsrc.at[k], rc.at[k], tc_ss.at[k], tc_rs.at[k], other)

    def tx_copy(k):
        return copy(sx.at[k], rx.at[k - 1], tx_ss.at[0], tx_rs.at[0], xp(k))

    def settle(k):
        tc_copy(k).wait_recv()
        t = town[k] + rc[k].astype(F32)
        if k:
            sx[k] = t.astype(BF16)
            tx_copy(k).start()
        else:
            town[k] = t

    turns = (2, 1, 3, 0)
    for p, k in enumerate(turns):
        s = ((x + k) % NX) * 2
        weigh(s + oc)
        weigh(s + c)
        tsrc[k] = spread(s + oc).astype(BF16)
        tc_copy(k).start()
        if p:
            settle(turns[p - 1])
        town[k] = spread(s + c)
    settle(0)

    acc = dot(gall[0], xall[0], 1, 0)
    for s in range(1, SLOTS):
        acc = acc + dot(gall[s], xall[s], 1, 0)
    qv[...] = norm_vjp(qraw[...], acc * INV_TEMPER).astype(BF16)

    landed(hz.at[pl.ds(0, NZ - 1)], hz_rs.at[0])
    hv = hz[...].astype(F32)
    hv = jnp.concatenate([hv[:, :8, :].reshape(64, 512), hv[:, 8:, :].reshape(64, 512)], axis=1)
    hv = hv.astype(BF16)
    for i in range(NY):
        hsrc[i] = hv[:, i * ROWS : (i + 1) * ROWS]
    hcol[y] = hsrc[y]
    for k in range(1, NY):
        copy(hsrc.at[(y + k) % NY], hcol.at[y], hy_ss.at[0], hy_rs.at[0], yp(k)).start()
    left_here(hcol.at[pl.ds(0, NY - 1)], hy_ss.at[0])
    picked = jnp.sum(psum[...], axis=1, keepdims=True)
    sums = jnp.sum(esum[...], axis=1, keepdims=True)
    loss = (jnp.log2(sums) - picked) * (1.0 / LOG2E)
    loss = jnp.broadcast_to(loss, (TOK, HALF)).reshape(TOK // HALF, HALF, HALF)
    down = lax.broadcasted_iota(jnp.int32, (TOK // HALF, HALF, HALF), 1)
    across = lax.broadcasted_iota(jnp.int32, (TOK // HALF, HALF, HALF), 2)
    loss_ref[...] = jnp.sum(jnp.where(down == across, loss, 0.0), axis=1)

    qfull[...] = dot(hq[...], qv[...], 0, 0)

    def core_rows(i, core):
        return pl.ds(pl.multiple_of(i * ROWS + core * HALF, HALF), HALF)

    for i in range(NY):
        qsrc[i] = qfull[core_rows(i, oc), :].astype(BF16)
    qc_cp = push(qsrc, qrc, qc_ss.at[0], qc_rs.at[0], other)

    flush()
    for k in range(1, NX):
        sent.append(vx_copy(k))
    for k in range(NX):
        sent.append(vc_copy(k))
        sent.append(tc_copy(k))
    left_here(rx, tx_ss.at[0])
    landed(rx, tx_rs.at[0])
    t = town[0]
    for k in range(NX - 1):
        t = t + rx[k].astype(F32)
    sg[...] = stack(t).astype(BF16)
    for i in range(len(plane)):
        copy(sg.at[pg(i)], rg.at[i], tp_ss.at[0], tp_rs.at[0], pp(i)).start()

    qc_cp.wait_recv()
    for i in range(NY):
        q = qfull[core_rows(i, c), :] + qrc[i].astype(F32)
        qsx[:, i] = q.reshape(NX, LINE, DOUT).astype(BF16)
    for k in (1, 3, 2):
        copy(qsx.at[(x + k) % NX], qrx.at[k - 1], qx_ss.at[0], qx_rs.at[0], xp(k)).start()
    flush()
    left_here(rg, tp_ss.at[0])
    left_here(qrx, qx_ss.at[0])

    landed(rg, tp_rs.at[0])
    t = sg[mine].astype(F32)
    for i in range(len(plane)):
        t = t + rg[i].astype(F32)
    t = jnp.concatenate([t[:8], t[8:]], axis=1)
    rgv[mine] = stack(norm_vjp(iraw, t))[0].astype(BF16)
    for i in range(len(plane)):
        copy(rgv.at[mine], rgv.at[mine], gp_ss.at[0], gp_rs.at[0], pp(i)).start()

    landed(qrx, qx_rs.at[0])
    q = qsx[x].astype(F32)
    for k in range(NX - 1):
        q = q + qrx[k].astype(F32)
    qsy[...] = q.astype(BF16)
    for k in range(1, NY):
        copy(qsy.at[(y + k) % NY], qry.at[k - 1], qy_ss.at[0], qy_rs.at[0], yp(k)).start()
    flush()
    left_here(rgv.at[pl.ds(0, PLANE - 1)], gp_ss.at[0])
    left_here(qry, qy_ss.at[0])

    landed(qry, qy_rs.at[0])
    q = qsy[y].astype(F32)
    for k in range(NY - 1):
        q = q + qry[k].astype(F32)
    qz[z] = q.astype(BF16)
    for k in Z_FAR:
        copy(qz.at[z], qz.at[z], qz_ss.at[0], qz_rs.at[0], zp(k)).start()
    left_here(qz.at[pl.ds(0, NZ - 1)], qz_ss.at[0])

    landed(hcol.at[pl.ds(0, NY - 1)], hy_rs.at[0])
    landed(rgv.at[pl.ds(0, PLANE - 1)], gp_rs.at[0])
    left, right = unstack(rgv[...].astype(F32))
    raw_grad = jnp.concatenate([left, right], axis=1).astype(BF16)
    aown[...] = dot(hcol[...].reshape(BLOCK, ROWS), raw_grad, 0, 0)
    ac_cp = push(aown.at[core_rows(0, oc)], arc, ac_ss.at[0], ac_rs.at[0], other)

    ac_cp.wait_recv()
    asx[...] = (aown[core_rows(0, c), :] + arc[...]).reshape(NX, LINE, DOUT)
    for k in (2, 1, 3):
        copy(asx.at[(x + k) % NX], arx.at[k - 1], ax_ss.at[0], ax_rs.at[0], xp(k)).start()
    flush()
    left_here(arx, ax_ss.at[0])

    def square_sum(m):
        v = fin[m][...].reshape(HID, DOUT).astype(F32)
        v = jnp.sum((v * v).reshape(HID // 8, 8, DOUT), axis=0)
        return v[:, :HALF] + v[:, HALF:]

    def group(ref, ky, lead):
        return ref.at[lead + (pl.ds(0, NX - 1),)] if ky == 0 else ref.at[lead]

    def gather(m):
        for kx, ky in sheet:
            copy(
                fin[m].at[y, c, x], fin[m].at[y, c, x], f_ss.at[m, ky], f_rs.at[m, ky], sp(kx, ky)
            ).start()
        for ky in range(NY):
            left_here(group(fin[m], ky, (0, 0)), f_ss.at[m, ky])

    def gather_core(m):
        for ky in range(NY):
            landed(group(fin[m], ky, (0, 0)), f_rs.at[m, ky])
            block = fin[m].at[(y + NY - ky) % NY, c]
            fc_cp.append(push(block, block, fc_ss.at[m, ky], fc_rs.at[m, ky], other))

    fc_cp = []

    landed(qz.at[pl.ds(0, NZ - 1)], qz_rs.at[0])
    q = qz[0].astype(F32)
    for k in range(1, NZ):
        q = q + qz[k].astype(F32)
    fin_query[y, c, x] = q.astype(BF16)
    gather(0)

    landed(arx, ax_rs.at[0])
    a = asx[x]
    for k in range(NX - 1):
        a = a + arx[k]
    fin_item[y, c, x] = a.astype(BF16)
    gather(1)
    gather_core(0)
    flush()
    for cp in fc_cp:
        cp.wait_recv()
    square = square_sum(0)
    gather_core(1)
    for cp in fc_cp[NY:]:
        cp.wait_recv()
    square = square + square_sum(1)
    square = jnp.sum(square, axis=0, keepdims=True)
    norm = jnp.sqrt(jnp.sum(square, axis=1, keepdims=True))
    limit = (HID * DOUT / 2) ** 0.5
    factor_ref[...] = jnp.broadcast_to(limit / jnp.maximum(norm, limit), (1, DOUT))
    flush()


def finish(loss_in, query_in, item_in, factor_in, loss_out, query_out, item_out):
    loss_out[...] = loss_in[...]
    query_out[...] = query_in[...].reshape(HID, DOUT).astype(F32) * factor_in[...]
    item_out[...] = item_in[...].reshape(HID, DOUT).astype(F32) * factor_in[...]


def local(
    user_features, w_query_in, w_query_out, quo_table, rem_table, w_item_in, w_item_out,
    quo_bucket, rem_bucket, counts, positive,
):
    def vm(*shape, dtype=BF16):
        return pltpu.VMEM(shape, dtype)

    def dma(*shape):
        return [pltpu.SemaphoreType.DMA(shape)] * 2

    anyspace = pl.BlockSpec(memory_space=pl.ANY)
    vmem = pl.BlockSpec(memory_space=pltpu.VMEM)
    scratch = [
        pltpu.SMEM((BLOCK // 8,), jnp.int32), pltpu.SMEM((BLOCK // 8,), jnp.int32),
        vm(16, HALF, dtype=jnp.int32), vm(TOK // HALF, HALF, dtype=jnp.int32),
        vm(TOK, DIN), vm(DIN, HID), vm(HID, DOUT), vm(CHUNKS, 4 * SHARD, WIDE), vm(DIN, HID), vm(HID, DOUT),
        vm(NY, HALF, dtype=jnp.int32), vm(PLANE - 1, NY, HALF, dtype=jnp.int32), vm(NY, HALF, 4 * SHARD),
        vm(CHUNKS - 1, NY, HALF, WIDE), vm(CHUNKS - 1, NY - 1, HALF, WIDE),
        vm(CHUNKS - 1, NZ, 16, WIDE), vm(CHUNKS - 1, NZ - 1, 16, WIDE),
        vm(NZ, NY * 16, WIDE), vm(NZ - 1, NY * 16, WIDE), vm(NY, 16, WIDE), vm(NY - 1, 16, WIDE),
        vm(16, HID, dtype=F32),
        vm(TOK, HID), vm(TOK, DOUT, dtype=F32), vm(TOK, DOUT),
        vm(SLOTS, BLOCK, DOUT), vm(PLANE, 16, HALF), vm(NZ, 16, 512), vm(NY, 64, ROWS), vm(NY, 64, ROWS),
        vm(SLOTS, TOK, BLOCK, dtype=F32), vm(TOK, HALF, dtype=F32), vm(TOK, HALF, dtype=F32),
        vm(TOK, HALF, dtype=jnp.int32), vm(TOK, HALF, dtype=F32), vm(SLOTS, TOK, BLOCK),
        vm(NX, BLOCK, DOUT), vm(NX, BLOCK, DOUT), vm(NX, BLOCK, DOUT), vm(NX - 1, BLOCK, DOUT),
        vm(NX, BLOCK, DOUT, dtype=F32), vm(PLANE, 16, HALF), vm(PLANE - 1, 16, HALF),
        vm(PLANE, 16, HALF), vm(HALF, DOUT, dtype=F32), vm(ROWS, DOUT, dtype=F32),
        vm(NX, LINE, DOUT, dtype=F32), vm(NX - 1, LINE, DOUT, dtype=F32),
        vm(HID, DOUT, dtype=F32), vm(NY, HALF, DOUT), vm(NY, HALF, DOUT),
        vm(NX, NY, LINE, DOUT), vm(NX - 1, NY, LINE, DOUT), vm(NY, LINE, DOUT), vm(NY - 1, LINE, DOUT),
        vm(NZ, LINE, DOUT),
        vm(SLOTS, 1, BLOCK, dtype=F32),
        pltpu.SemaphoreType.DMA((2 * CHUNKS + 9,)),
        *dma(1), *dma(2, CHUNKS), *dma(CHUNKS - 1), *dma(CHUNKS - 1), *dma(1), *dma(1),
        *dma(1), *dma(3), *dma(4),
        *dma(1), *dma(1),
        *dma(4), *dma(1), *dma(1),
        *dma(1),
        *dma(1), *dma(1),
        *dma(1), *dma(1), *dma(1), *dma(1),
        *dma(2, 4), *dma(2, 4),
    ]
    losses, grad_query, grad_item, factor = pl.pallas_call(
        kernel,
        out_shape=(
            jax.ShapeDtypeStruct((TOK // HALF, HALF), F32),
            jax.ShapeDtypeStruct((NY, NC, NX, LINE, DOUT), BF16),
            jax.ShapeDtypeStruct((NY, NC, NX, LINE, DOUT), BF16),
            jax.ShapeDtypeStruct((1, DOUT), F32),
        ),
        in_specs=[anyspace] * 11,
        out_specs=(vmem, vmem, vmem, vmem),
        scratch_shapes=scratch,
        compiler_params=pltpu.CompilerParams(
            collective_id=0, has_side_effects=True, vmem_limit_bytes=56 * 2**20
        ),
        cost_estimate=pl.CostEstimate(flops=6_500_000_000, bytes_accessed=12_000_000, transcendentals=2_100_000),
        name="step",
    )(
        quo_bucket, rem_bucket, user_features, w_query_in, w_query_out, quo_table, rem_table, w_item_in,
        w_item_out, counts.reshape(16, HALF), positive.reshape(TOK // HALF, HALF),
    )
    losses, grad_query, grad_item = pl.pallas_call(
        finish,
        out_shape=(
            jax.ShapeDtypeStruct((TOK // HALF, HALF), F32),
            jax.ShapeDtypeStruct((HID, DOUT), F32),
            jax.ShapeDtypeStruct((HID, DOUT), F32),
        ),
        in_specs=[vmem] * 4,
        out_specs=(vmem, vmem, vmem),
        name="scale",
    )(losses, grad_query, grad_item, factor)
    return (losses.reshape(TOK), grad_query, grad_item)


def solution(mesh):
    in_specs = (
        P(("sec", "dev"), None), P(), P(), P("dev", None), P("dev", None), P(), P(),
        P("dev"), P("dev"), P(), P(("sec", "dev")),
    )
    out_specs = (P(("sec", "dev")), P(), P())
    return jax.shard_map(local, mesh=mesh, in_specs=in_specs, out_specs=out_specs, check_vma=False)
```
